512 devices in a mesh: src: 8 (over y_hi, x), space: 64 (over z, y_lo, core).
Axes of the slice: x: 4, y: 4 (y_hi: 2, y_lo: 2; y = y_hi * 2 + y_lo), z: 16, core: 2. Of those that a mesh axis runs over, the one named last changes fastest.
Arguments:
- propagators: bfloat16 [64, 2, 144, 8192], P('src', None, None, 'space'), may hold values from -1.5 to 1.5
- source_coords: int32 [64, 3], replicated, may hold values from 0 to 95
- momenta: int32 [33, 3], replicated, may hold values from -2 to 2
- slab_start: int32 [1], replicated, may hold values from 0 to 884735
Outputs:
- correlator: float32 [64, 64, 2, 33], P('src', 'space')
The draws below stay inside these ranges and needn't reach their ends.
All inputs are finite; a program needn't handle non-finite values.
Results may differ from the reference program's by a relative error of at most 0.0026.
Values may be sent and summed in bfloat16 or wider, within the bound.
A program may use at most 64 MiB of HBM per device.

```python
import math
import jax
import jax.numpy as jnp
from jax import lax

NC = 12
LAT = 96
NMOM = 33
SITES_DEV = 128
NSRC = 64
NSITES = 8192


def plant(result, own_key, low, largest):
    longest = result.shape.index(max(result.shape))
    spots = []
    for shift in (0, 1):
        where = [jax.random.randint(jax.random.fold_in(own_key, axis), (), 0, length) for axis, length in enumerate(result.shape)]
        where[longest] = (where[longest] + shift) % result.shape[longest]
        spots.append(tuple(where))
    return result.at[spots[0]].set(low).at[spots[1]].set(largest)


def block_levels(rng, shape, pieces, least, top_value):
    def one(axis_at, shards_of):
        draws = jax.random.uniform(jax.random.fold_in(jax.random.fold_in(rng, 6), axis_at), (shards_of,), jnp.float32, least / len(pieces), top_value / len(pieces))
        return jnp.repeat(jnp.exp(draws), shape[axis_at] // shards_of).reshape((-1,) + (1,) * (len(shape) - axis_at - 1))

    loudness = one(*pieces[0])
    for cut in pieces[1:]:
        loudness = loudness * one(*cut)
    return loudness


def centred(rng, extent, scale, reach, shards=(), held_as=jnp.bfloat16):
    array = scale * jax.random.normal(rng, extent, jnp.float32)
    if shards:
        array = array * block_levels(rng, extent, shards, -0.22, 0.18)
    return jnp.clip(array, -reach, reach).astype(held_as)


def setup_inputs(seed: int = 0) -> dict:
    seeds = jax.random.split(jax.random.key(seed), 5)
    propagators = centred(seeds[0], (NSRC, 2, NC * NC, NSITES), 0.25, 1.5, ((0, 8), (3, 64)))
    source_coords = plant(jax.random.randint(seeds[1], (NSRC, 3), 0, LAT), jax.random.fold_in(seeds[1], 1), 0, LAT - 1).astype(jnp.int32)
    momenta = plant(jax.random.randint(seeds[2], (NMOM, 3), -2, 3), jax.random.fold_in(seeds[2], 1), -2, 2).astype(jnp.int32)
    slab_start = jax.random.randint(seeds[3], (1,), 0, LAT * LAT * LAT).astype(jnp.int32)
    return {"propagators": propagators, "source_coords": source_coords, "momenta": momenta, "slab_start": slab_start}


def phase_table(site_index, momenta):
    cube = LAT * LAT * LAT
    glob = jnp.mod(site_index, cube)
    first = glob // (LAT * LAT)
    second = jnp.mod(glob // LAT, LAT)
    third = jnp.mod(glob, LAT)
    dotted = first[:, None] * momenta[None, :, 0] + second[:, None] * momenta[None, :, 1] + third[:, None] * momenta[None, :, 2]
    angle = jnp.mod(dotted, LAT).astype(jnp.float32) * jnp.float32(2.0 * math.pi / LAT)
    return jnp.concatenate([jnp.cos(angle), jnp.sin(angle)], axis=1).astype(jnp.bfloat16)

def pair_traces(left, right):
    count_a = left.shape[0]
    count_b = right.shape[0]
    width = left.shape[3]
    left32 = left.astype(jnp.float32)
    right32 = right.astype(jnp.float32)
    hp = lax.Precision.HIGHEST
    real_part = jnp.einsum('akx,bkx->abx', left32.reshape(count_a, -1, width), right32.reshape(count_b, -1, width), precision=hp)
    imag_part = jnp.einsum('acx,bcx->abx', left32[:, 0], right32[:, 1], precision=hp) - jnp.einsum('acx,bcx->abx', left32[:, 1], right32[:, 0], precision=hp)
    return jnp.stack([real_part, imag_part], axis=2).astype(jnp.bfloat16)

def project(pair_trace, phases):
    count_a, count_b, two, width = pair_trace.shape
    moms = phases.shape[1] // 2
    prod = jnp.dot(pair_trace.reshape(-1, width), phases, preferred_element_type=jnp.float32)
    prod = prod.reshape(count_a, count_b, 2, 2, moms)
    real_part = prod[:, :, 0, 0] + prod[:, :, 1, 1]
    imag_part = prod[:, :, 1, 0] - prod[:, :, 0, 1]
    return jnp.stack([real_part, imag_part], axis=2)

def finish(raw, coords, momenta, total_sites):
    dotted = jnp.mod(coords @ momenta.T, LAT)
    angle = dotted.astype(jnp.float32) * jnp.float32(2.0 * math.pi / LAT)
    cosine = jnp.cos(angle)[None, :, :]
    sine = jnp.sin(angle)[None, :, :]
    real_part = raw[:, :, 0]
    imag_part = raw[:, :, 1]
    scale = jnp.float32(1.0 / math.sqrt(total_sites))
    new_real = (real_part * cosine - imag_part * sine) * scale
    new_imag = (real_part * sine + imag_part * cosine) * scale
    return jnp.stack([new_real, new_imag], axis=2)

def reference(propagators, source_coords, momenta, slab_start):
    blocks = NSITES // SITES_DEV

    def step(carry, block):
        begin = (block * SITES_DEV).astype(jnp.int32)
        piece = lax.dynamic_slice_in_dim(propagators, begin, SITES_DEV, 3)
        site_index = slab_start[0] + begin + jnp.arange(SITES_DEV, dtype=jnp.int32)
        phases = phase_table(site_index, momenta)
        return (carry + project(pair_traces(piece, piece), phases), None)
    init = jnp.zeros((NSRC, NSRC, 2, NMOM), jnp.float32)
    raw, unused = lax.scan(step, init, jnp.arange(blocks, dtype=jnp.int32))
    return finish(raw, source_coords, momenta, NSITES)
```

```python
import functools
import math

import jax
import jax.numpy as jnp
from jax import lax
from jax.experimental import pallas as pl
from jax.experimental.pallas import tpu as pltpu
from jax.sharding import PartitionSpec as P

LAT = 96
NC2 = 144
K = 2 * NC2
NMOM = 33
NSRC_AX = 8
NQ = 4
NZ = 16
LANES = 128
MESH = pl.DeviceIdType.MESH
BF = jnp.bfloat16
F32 = jnp.float32


def swap_bits(vs, bits, lane):
    vs = list(vs)
    for bit, s in bits:
        low = (lane & s) == 0
        for u in range(len(vs)):
            if u & bit:
                continue
            a, b = vs[u], vs[u | bit]
            vs[u] = jnp.where(low, a, pltpu.roll(b, s, 1))
            vs[u | bit] = jnp.where(low, pltpu.roll(a, LANES - s, 1), b)
    return vs


def mod_lat(u):
    return u - LAT * jnp.floor((u + 0.5) * (1.0 / LAT))


def cos_steps(u):
    t = (jnp.abs(u - 48.0) - 24.0) * (2.0 * math.pi / LAT)
    t2 = t * t
    acc = jnp.full_like(t, 1.0 / math.factorial(13))
    for n in (11, 9, 7, 5, 3, 1):
        sign = 1.0 if n % 4 == 1 else -1.0
        acc = acc * t2 + sign / math.factorial(n)
    return acc * t


def kernel(
    prop, coords, momenta, slab, out,
    x_in, send1, recv1, lt, tt, gram, send2, recv2, lhs, wts, send3, recv3,
    in_sem, loc_sem, s1, r1, s2, r2, s3, r3,
):
    src = lax.axis_index("src")
    space = lax.axis_index("space")
    z = space // NQ
    q = space % NQ
    sx = src % 4
    sy = src // 4

    load = pltpu.make_async_copy(prop, x_in, in_sem)
    load.start()

    barrier = pltpu.get_barrier_semaphore()
    for r in range(1, NSRC_AX * NQ):
        dev = {"src": (src + r // NQ) % NSRC_AX, "space": z * NQ + (q + r) % NQ}
        pl.semaphore_signal(barrier, inc=1, device_id=dev, device_id_type=MESH)
    for r in range(1, NZ):
        dev = {"src": src, "space": ((z + r) % NZ) * NQ + q}
        pl.semaphore_signal(barrier, inc=1, device_id=dev, device_id_type=MESH)

    load.wait()
    lane16 = lax.broadcasted_iota(jnp.int32, (16, LANES), 1)
    for c in range(2):
        for t in range(NC2 // 16):
            vs = [x_in[b, c, t * 16 : t * 16 + 16, :] for b in range(8)]
            vs = swap_bits(vs, ((1, 1), (2, 2), (4, 4)), lane16)
            for d in range(8):
                row = c * NC2 + t * 16
                send1[d, row : row + 16, :] = vs[d]

    pl.semaphore_wait(barrier, NSRC_AX * NQ - 1 + NZ - 1)

    order = ((0, 1), (0, 3), (1, 0), (0, 2), (1, 1), (1, 3), (1, 2))
    own = pltpu.make_async_copy(send1.at[src], recv1.at[src], loc_sem.at[0])
    own.start()
    out1 = []
    for dy, dx in order:
        d = ((sy + dy) % 2) * 4 + (sx + dx) % 4
        cp = pltpu.make_async_remote_copy(
            src_ref=send1.at[d], dst_ref=recv1.at[src], send_sem=s1.at[d], recv_sem=r1.at[src],
            device_id={"src": d, "space": space}, device_id_type=MESH,
        )
        cp.start()
        out1.append(cp)

    lane1 = lax.broadcasted_iota(jnp.int32, (1, LANES), 1)
    first_half = lane1 < NMOM
    m3 = momenta[...].astype(F32)
    m3 = jnp.concatenate([m3, m3, jnp.zeros((3, LANES - 2 * NMOM), F32)], axis=1)
    base = slab[0] + z * (NQ * LANES)
    shift_a = jnp.where(first_half, 0.0, 24.0)
    shift_b = jnp.where(first_half, 72.0, 0.0)
    rows = 64

    def phases(step, carry):
        site = lax.broadcasted_iota(jnp.int32, (rows, LANES), 0) + (base + step * rows)
        site = jnp.where(site >= LAT * LAT * LAT, site - LAT * LAT * LAT, site).astype(F32)
        x0 = jnp.floor((site + 0.5) * (1.0 / (LAT * LAT)))
        rest = site - x0 * (LAT * LAT)
        x1 = jnp.floor((rest + 0.5) * (1.0 / LAT))
        x2 = rest - x1 * LAT
        u = x0 * m3[0:1] + x1 * m3[1:2] + x2 * m3[2:3]
        w = jnp.concatenate([cos_steps(mod_lat(u + shift_a)), cos_steps(mod_lat(u + shift_b))], axis=1)
        wts[pl.ds(pl.multiple_of(step * rows, rows), rows), :] = w.astype(BF)
        return carry

    lax.fori_loop(0, NQ * LANES // rows, phases, 0)

    def take(j):
        block = recv1[j]
        lt[pl.ds(pl.multiple_of(j * LANES, LANES), LANES), :] = block.T

    own.wait()
    take(src)
    for dy, dx in order:
        d = ((sy - dy + 2) % 2) * 4 + (sx - dx + 4) % 4
        pltpu.make_async_remote_copy(
            src_ref=send1.at[d], dst_ref=recv1.at[d], send_sem=s1.at[d], recv_sem=r1.at[d],
            device_id={"src": d, "space": space}, device_id_type=MESH,
        ).wait_recv()
        take(d)

    lane8 = lax.broadcasted_iota(jnp.int32, (8, LANES), 1) >> 3
    picks = [lane8 == x for x in range(16)]

    def columns(j, carry):
        block = recv1[j]
        turned = jnp.concatenate([block[NC2:], -block[:NC2]], axis=0)
        w = jnp.concatenate([block, turned], axis=1)
        tt[...] = jnp.dot(lt[...], w, preferred_element_type=F32)

        def pick(i, carry2):
            at = pl.multiple_of(i * LANES, LANES)
            parts = []
            for c in range(2):
                acc = jnp.zeros((8, LANES), F32)
                for x in range(16):
                    acc = jnp.where(picks[x], tt[pl.ds(at + 8 * x, 8), c * LANES : (c + 1) * LANES], acc)
                parts.append(acc)
            gram[i, j] = jnp.concatenate(parts, axis=0).astype(BF)
            return carry2

        lax.fori_loop(0, 8, pick, 0)
        return carry

    lax.fori_loop(0, 8, columns, 0)

    def split(i, carry):
        for jhi in range(2):
            vs = [gram[i, 4 * jhi + jlo] for jlo in range(4)]
            vs = swap_bits(vs, ((1, 1), (2, 2)), lane16)
            for t in range(4):
                send2[i * NQ + t, jhi * 16 : jhi * 16 + 16, :] = vs[t]
        return carry

    lax.fori_loop(0, 8, split, 0)

    me = src * NQ + q
    own2 = pltpu.make_async_copy(send2.at[me], recv2.at[me], loc_sem.at[1])
    own2.start()
    out2 = []
    for r in range(1, NSRC_AX * NQ):
        ds, dq = (src + r // NQ) % NSRC_AX, (q + r) % NQ
        to = ds * NQ + dq
        cp = pltpu.make_async_remote_copy(
            src_ref=send2.at[to], dst_ref=recv2.at[me], send_sem=s2.at[to], recv_sem=r2.at[me],
            device_id={"src": ds, "space": z * NQ + dq}, device_id_type=MESH,
        )
        cp.start()
        out2.append(cp)
    own2.wait()
    for r in range(1, NSRC_AX * NQ):
        ds, dq = (src - r // NQ + NSRC_AX) % NSRC_AX, (q - r % NQ + NQ) % NQ
        at = ds * NQ + dq
        pltpu.make_async_remote_copy(
            src_ref=send2.at[at], dst_ref=recv2.at[at], send_sem=s2.at[at], recv_sem=r2.at[at],
            device_id={"src": ds, "space": z * NQ + dq}, device_id_type=MESH,
        ).wait_recv()

    for qq in range(NQ):
        for jhi in range(2):
            vs = [recv2[d * NQ + qq, jhi * 16 : jhi * 16 + 16, :] for d in range(8)]
            vs = swap_bits(vs, ((1, 1), (2, 2), (4, 4)), lane16)
            for b in range(8):
                row = (jhi * 8 + b) * 16
                lhs[row : row + 16, qq * LANES : (qq + 1) * LANES] = vs[b]
    prod = jnp.dot(lhs[...], wts[...], preferred_element_type=F32)
    for b in range(16):
        zb = 8 * (b // 8) + 2 * (b % 4) + (b // 4) % 2
        send3[zb] = prod[b * 16 : b * 16 + 8, :LANES] + prod[b * 16 + 8 : b * 16 + 16, LANES:]

    own3 = pltpu.make_async_copy(send3.at[z], recv3.at[z], loc_sem.at[2])
    own3.start()
    out3 = []
    for r in range(1, NZ):
        to = (z + r) % NZ
        cp = pltpu.make_async_remote_copy(
            src_ref=send3.at[to], dst_ref=recv3.at[z], send_sem=s3.at[to], recv_sem=r3.at[z],
            device_id={"src": src, "space": to * NQ + q}, device_id_type=MESH,
        )
        cp.start()
        out3.append(cp)
    own3.wait()
    for r in range(1, NZ):
        at = (z - r + NZ) % NZ
        pltpu.make_async_remote_copy(
            src_ref=send3.at[at], dst_ref=recv3.at[at], send_sem=s3.at[at], recv_sem=r3.at[at],
            device_id={"src": src, "space": at * NQ + q}, device_id_type=MESH,
        ).wait_recv()
    total = recv3[0]
    for t in range(1, NZ):
        total = total + recv3[t]

    here = lax.broadcasted_iota(jnp.int32, (3, 64), 1) == space
    xyz = jnp.sum(jnp.where(here, coords[...].astype(F32), 0.0), axis=1, keepdims=True)
    u = jnp.sum(xyz * m3, axis=0, keepdims=True)
    scale = 1.0 / math.sqrt(NZ * NQ * LANES)
    cosine = cos_steps(mod_lat(u)) * scale
    sine = cos_steps(mod_lat(u + jnp.where(first_half, 24.0, 72.0))) * scale
    swapped = jnp.where(first_half, pltpu.roll(total, LANES - NMOM, 1), pltpu.roll(total, NMOM, 1))
    done = total * cosine + swapped * sine
    out[0, 0] = done[:, :NMOM]
    out[0, 1] = pltpu.roll(done, LANES - NMOM, 1)[:, :NMOM]

    for cp in out1 + out2 + out3:
        cp.wait_send()


def per_device(propagators, source_coords, momenta, slab_start):
    vm = pl.BlockSpec(memory_space=pltpu.VMEM)
    dma = pltpu.SemaphoreType.DMA
    result = pl.pallas_call(
        kernel,
        out_shape=jax.ShapeDtypeStruct((1, 2, 8, NMOM), F32),
        in_specs=[pl.BlockSpec(memory_space=pl.ANY), vm, vm, pl.BlockSpec(memory_space=pltpu.SMEM)],
        out_specs=vm,
        scratch_shapes=[
            pltpu.VMEM((8, 2, NC2, LANES), BF),
            pltpu.VMEM((8, K, LANES), BF),
            pltpu.VMEM((8, K, LANES), BF),
            pltpu.VMEM((8 * LANES, K), BF),
            pltpu.VMEM((8 * LANES, 2 * LANES), F32),
            pltpu.VMEM((8, 8, 16, LANES), BF),
            pltpu.VMEM((32, 32, LANES), BF),
            pltpu.VMEM((32, 32, LANES), BF),
            pltpu.VMEM((256, NQ * LANES), BF),
            pltpu.VMEM((NQ * LANES, 2 * LANES), BF),
            pltpu.VMEM((NZ, 8, LANES), F32),
            pltpu.VMEM((NZ, 8, LANES), F32),
            dma,
            dma((3,)),
            dma((8,)),
            dma((8,)),
            dma((32,)),
            dma((32,)),
            dma((16,)),
            dma((16,)),
        ],
        compiler_params=pltpu.CompilerParams(
            collective_id=0, has_side_effects=True, vmem_limit_bytes=32 * 1024 * 1024
        ),
    )(propagators, source_coords.T, momenta.T, slab_start)
    return jnp.transpose(result, (2, 0, 1, 3))


def solution(mesh):
    placed = (P("src", None, None, "space"), P(), P(), P())
    return jax.shard_map(
        per_device,
        mesh=mesh,
        in_specs=placed,
        out_specs=P("src", "space", None, None),
        check_vma=False,
    )
```

```python
import functools
import math

import jax
import jax.numpy as jnp
from jax import lax
from jax.experimental import pallas as pl
from jax.experimental.pallas import tpu as pltpu
from jax.sharding import PartitionSpec as P

LAT = 96
NC2 = 144
K = 2 * NC2
NMOM = 33
NSRC_AX = 8
NQ = 4
NZ = 16
LANES = 128
MESH = pl.DeviceIdType.MESH
BF = jnp.bfloat16
F32 = jnp.float32


def swap_bits(vs, bits, lane):
    vs = list(vs)
    for bit, s in bits:
        low = (lane & s) == 0
        for u in range(len(vs)):
            if u & bit:
                continue
            a, b = vs[u], vs[u | bit]
            vs[u] = jnp.where(low, a, pltpu.roll(b, s, 1))
            vs[u | bit] = jnp.where(low, pltpu.roll(a, LANES - s, 1), b)
    return vs


def mod_lat(u):
    return u - LAT * jnp.floor((u + 0.5) * (1.0 / LAT))


def cos_steps(u):
    t = (jnp.abs(u - 48.0) - 24.0) * (2.0 * math.pi / LAT)
    t2 = t * t
    acc = jnp.full_like(t, 1.0 / math.factorial(13))
    for n in (11, 9, 7, 5, 3, 1):
        sign = 1.0 if n % 4 == 1 else -1.0
        acc = acc * t2 + sign / math.factorial(n)
    return acc * t


def kernel(
    prop, coords_any, momenta_any, slab_any, out,
    x_in, coords, momenta, slab, send1, recv1, lt, wg, send2, recv2, lhs, wts, send3, recv3,
    in_sem, loc_sem, s1, r1, s2, r2, s3, r3,
):
    src = lax.axis_index("src")
    space = lax.axis_index("space")
    z = space // NQ
    q = space % NQ
    sx = src % 4
    sy = src // 4

    loads = [pltpu.make_async_copy(prop.at[:, c], x_in.at[:, c], in_sem.at[c]) for c in range(2)]
    small = [
        pltpu.make_async_copy(slab_any, slab, in_sem.at[2]),
        pltpu.make_async_copy(momenta_any, momenta, in_sem.at[3]),
        pltpu.make_async_copy(coords_any, coords, in_sem.at[4]),
    ]
    for cp in loads + small:
        cp.start()

    barrier = pltpu.get_barrier_semaphore()
    for r in range(1, NSRC_AX * NQ):
        dev = {"src": (src + r // NQ) % NSRC_AX, "space": z * NQ + (q + r) % NQ}
        pl.semaphore_signal(barrier, inc=1, device_id=dev, device_id_type=MESH)
    for r in range(1, NZ):
        dev = {"src": src, "space": ((z + r) % NZ) * NQ + q}
        pl.semaphore_signal(barrier, inc=1, device_id=dev, device_id_type=MESH)

    lane16 = lax.broadcasted_iota(jnp.int32, (16, LANES), 1)
    for c in range(2):
        loads[c].wait()
        for t in range(NC2 // 16):
            vs = [x_in[b, c, t * 16 : t * 16 + 16, :] for b in range(8)]
            vs = swap_bits(vs, ((1, 1), (2, 2), (4, 4)), lane16)
            for d in range(8):
                row = c * NC2 + t * 16
                send1[d, row : row + 16, :] = vs[d]

    pl.semaphore_wait(barrier, NSRC_AX * NQ - 1 + NZ - 1)

    order = ((0, 1), (0, 3), (1, 0), (0, 2), (1, 1), (1, 3), (1, 2))
    own = pltpu.make_async_copy(send1.at[src], recv1.at[src], loc_sem.at[0])
    own.start()
    sent = []
    for dy, dx in order:
        d = ((sy + dy) % 2) * 4 + (sx + dx) % 4
        cp = pltpu.make_async_remote_copy(
            src_ref=send1.at[d], dst_ref=recv1.at[src], send_sem=s1.at[d], recv_sem=r1.at[src],
            device_id={"src": d, "space": space}, device_id_type=MESH,
        )
        cp.start()
        sent.append(cp)

    for cp in small:
        cp.wait()
    lane1 = lax.broadcasted_iota(jnp.int32, (1, LANES), 1)
    first_half = lane1 < NMOM
    m3 = momenta[...].astype(F32)
    m3 = jnp.concatenate([m3, m3, jnp.zeros((3, LANES - 2 * NMOM), F32)], axis=1)
    base = slab[0] + z * (NQ * LANES)
    shift_a = jnp.where(first_half, 0.0, 24.0)
    shift_b = jnp.where(first_half, 72.0, 0.0)
    rows = 64

    def phases(step, carry):
        row = lax.broadcasted_iota(jnp.int32, (rows, LANES), 0) + step * rows
        local = ((row >> 7) << 7) + (((row >> 5) & 3) << 1) + ((row >> 2) & 1) + (((row >> 3) & 3) << 3) + ((row & 3) << 5)
        site = local + base
        site = jnp.where(site >= LAT * LAT * LAT, site - LAT * LAT * LAT, site).astype(F32)
        x0 = jnp.floor((site + 0.5) * (1.0 / (LAT * LAT)))
        rest = site - x0 * (LAT * LAT)
        x1 = jnp.floor((rest + 0.5) * (1.0 / LAT))
        x2 = rest - x1 * LAT
        u = x0 * m3[0:1] + x1 * m3[1:2] + x2 * m3[2:3]
        w = jnp.concatenate([cos_steps(mod_lat(u + shift_a)), cos_steps(mod_lat(u + shift_b))], axis=1)
        wts[pl.ds(pl.multiple_of(step * rows, rows), rows), :] = w.astype(BF)
        return carry

    lax.fori_loop(0, NQ * LANES // rows, phases, 0)

    here = lax.broadcasted_iota(jnp.int32, (3, 64), 1) == space
    xyz = jnp.sum(jnp.where(here, coords[...].astype(F32), 0.0), axis=1, keepdims=True)
    u = jnp.sum(xyz * m3, axis=0, keepdims=True)
    scale = 1.0 / math.sqrt(NZ * NQ * LANES)
    cosine = cos_steps(mod_lat(u)) * scale
    sine = cos_steps(mod_lat(u + jnp.where(first_half, 24.0, 72.0))) * scale

    def take(j):
        turned = recv1[j].T
        for g in range(4):
            lt[g, pl.ds(pl.multiple_of(j * 32, 32), 32), :] = turned[g * 32 : g * 32 + 32]

    own.wait()
    take(src)
    for dy, dx in order:
        d = ((sy - dy + 2) % 2) * 4 + (sx - dx + 4) % 4
        pltpu.make_async_remote_copy(
            src_ref=send1.at[d], dst_ref=recv1.at[d], send_sem=s1.at[d], recv_sem=r1.at[d],
            device_id={"src": d, "space": space}, device_id_type=MESH,
        ).wait_recv()
        take(d)

    me = src * NQ + q
    lane8 = (lax.broadcasted_iota(jnp.int32, (8, LANES), 1) >> 3) & 3
    picks = [lane8 == x for x in range(4)]

    for jhi in range(2):
        for t in range(K // 16):
            at = t * 16
            vs = [recv1[4 * jhi + jlo, at : at + 16, :] for jlo in range(4)]
            vs = swap_bits(vs, ((1, 32), (2, 64)), lane16)
            for g in range(4):
                wg[g, at : at + 16, :LANES] = vs[g]
                if at < NC2:
                    wg[g, NC2 + at : NC2 + at + 16, LANES:] = -vs[g]
                else:
                    wg[g, at - NC2 : at - NC2 + 16, LANES:] = vs[g]
        traces = []
        for g in range(4):
            tt = jnp.dot(lt[g], wg[g], preferred_element_type=F32)
            for i in range(8):
                parts = []
                for c in range(2):
                    acc = tt[i * 32 : i * 32 + 8, c * LANES : (c + 1) * LANES]
                    for x in range(1, 4):
                        acc = jnp.where(picks[x], tt[i * 32 + 8 * x : i * 32 + 8 * x + 8, c * LANES : (c + 1) * LANES], acc)
                    parts.append(acc)
                traces.append(jnp.concatenate(parts, axis=0).astype(BF))
        for i in range(8):
            vs = swap_bits([traces[g * 8 + i] for g in range(4)], ((1, 1), (2, 2)), lane16)
            for t in range(4):
                send2[jhi, i * NQ + t] = vs[t]
        cp = pltpu.make_async_copy(send2.at[jhi, me], recv2.at[jhi, me], loc_sem.at[1 + jhi])
        cp.start()
        for r in range(1, NSRC_AX * NQ):
            ds, dq = (src + r // NQ) % NSRC_AX, (q + r) % NQ
            to = ds * NQ + dq
            cp = pltpu.make_async_remote_copy(
                src_ref=send2.at[jhi, to], dst_ref=recv2.at[jhi, me], send_sem=s2.at[jhi, to], recv_sem=r2.at[jhi, me],
                device_id={"src": ds, "space": z * NQ + dq}, device_id_type=MESH,
            )
            cp.start()
            sent.append(cp)

    for jhi in range(2):
        pltpu.make_async_copy(send2.at[jhi, me], recv2.at[jhi, me], loc_sem.at[1 + jhi]).wait()
        for r in range(1, NSRC_AX * NQ):
            ds, dq = (src - r // NQ + NSRC_AX) % NSRC_AX, (q - r % NQ + NQ) % NQ
            at = ds * NQ + dq
            pltpu.make_async_remote_copy(
                src_ref=send2.at[jhi, at], dst_ref=recv2.at[jhi, at], send_sem=s2.at[jhi, at], recv_sem=r2.at[jhi, at],
                device_id={"src": ds, "space": z * NQ + dq}, device_id_type=MESH,
            ).wait_recv()
        for qq in range(NQ):
            vs = [recv2[jhi, d * NQ + qq] for d in range(8)]
            vs = swap_bits(vs, ((1, 4), (2, 32), (4, 64)), lane16)
            for b in range(8):
                lhs[b * 16 : b * 16 + 16, qq * LANES : (qq + 1) * LANES] = vs[b]
        prod = jnp.dot(lhs[...], wts[...], preferred_element_type=F32)
        for b in range(8):
            send3[8 * jhi + b] = prod[b * 16 : b * 16 + 8, :LANES] + prod[b * 16 + 8 : b * 16 + 16, LANES:]
        for b in range(8):
            to = 8 * jhi + b

            @pl.when(z != to)
            def _():
                pltpu.make_async_remote_copy(
                    src_ref=send3.at[to], dst_ref=recv3.at[z], send_sem=s3.at[to], recv_sem=r3.at[z],
                    device_id={"src": src, "space": to * NQ + q}, device_id_type=MESH,
                ).start()

            @pl.when(z == to)
            def _():
                pltpu.make_async_copy(send3.at[to], recv3.at[to], loc_sem.at[3]).start()

    pltpu.make_async_copy(send3.at[z], recv3.at[z], loc_sem.at[3]).wait()
    for r in range(1, NZ):
        at = (z + r) % NZ
        cp = pltpu.make_async_remote_copy(
            src_ref=send3.at[at], dst_ref=recv3.at[at], send_sem=s3.at[at], recv_sem=r3.at[at],
            device_id={"src": src, "space": at * NQ + q}, device_id_type=MESH,
        )
        cp.wait_recv()
        sent.append(cp)
    total = recv3[0]
    for t in range(1, NZ):
        total = total + recv3[t]
    swapped = jnp.where(first_half, pltpu.roll(total, LANES - NMOM, 1), pltpu.roll(total, NMOM, 1))
    done = total * cosine + swapped * sine
    out[0, 0] = done[:, :NMOM]
    out[0, 1] = pltpu.roll(done, LANES - NMOM, 1)[:, :NMOM]

    for cp in sent:
        cp.wait_send()


def per_device(propagators, source_coords, momenta, slab_start):
    dma = pltpu.SemaphoreType.DMA
    result = pl.pallas_call(
        kernel,
        out_shape=jax.ShapeDtypeStruct((1, 2, 8, NMOM), F32),
        in_specs=[pl.BlockSpec(memory_space=pltpu.HBM)] * 4,
        out_specs=pl.BlockSpec(memory_space=pltpu.VMEM),
        scratch_shapes=[
            pltpu.VMEM((8, 2, NC2, LANES), BF),
            pltpu.VMEM((3, 64), jnp.int32),
            pltpu.VMEM((3, NMOM), jnp.int32),
            pltpu.SMEM((1,), jnp.int32),
            pltpu.VMEM((8, K, LANES), BF),
            pltpu.VMEM((8, K, LANES), BF),
            pltpu.VMEM((4, 256, K), BF),
            pltpu.VMEM((4, K, 2 * LANES), BF),
            pltpu.VMEM((2, 32, 16, LANES), BF),
            pltpu.VMEM((2, 32, 16, LANES), BF),
            pltpu.VMEM((LANES, NQ * LANES), BF),
            pltpu.VMEM((NQ * LANES, 2 * LANES), BF),
            pltpu.VMEM((NZ, 8, LANES), F32),
            pltpu.VMEM((NZ, 8, LANES), F32),
            dma((5,)),
            dma((4,)),
            dma((8,)),
            dma((8,)),
            dma((2, 32)),
            dma((2, 32)),
            dma((16,)),
            dma((16,)),
        ],
        compiler_params=pltpu.CompilerParams(
            collective_id=0, has_side_effects=True, vmem_limit_bytes=60 * 1024 * 1024
        ),
    )(propagators, source_coords.T, momenta.T, slab_start)
    return jnp.transpose(result, (2, 0, 1, 3))


def solution(mesh):
    placed = (P("src", None, None, "space"), P(), P(), P())
    return jax.shard_map(
        per_device,
        mesh=mesh,
        in_specs=placed,
        out_specs=P("src", "space", None, None),
        check_vma=False,
    )
```

```python
import functools
import math

import jax
import jax.numpy as jnp
from jax import lax
from jax.experimental import pallas as pl
from jax.experimental.pallas import tpu as pltpu
from jax.sharding import PartitionSpec as P

LAT = 96
NC2 = 144
K = 2 * NC2
NMOM = 33
NSRC_AX = 8
NQ = 4
NZ = 16
LANES = 128
MESH = pl.DeviceIdType.MESH
BF = jnp.bfloat16
F32 = jnp.float32


def swap_bits(vs, bits, lane):
    vs = list(vs)
    for bit, s in bits:
        low = (lane & s) == 0
        for u in range(len(vs)):
            if u & bit:
                continue
            a, b = vs[u], vs[u | bit]
            vs[u] = jnp.where(low, a, pltpu.roll(b, s, 1))
            vs[u | bit] = jnp.where(low, pltpu.roll(a, LANES - s, 1), b)
    return vs


def mod_lat(u):
    return u - LAT * jnp.floor((u + 0.5) * (1.0 / LAT))


def cos_steps(u):
    t = (jnp.abs(u - 48.0) - 24.0) * (2.0 * math.pi / LAT)
    t2 = t * t
    acc = jnp.full_like(t, 1.0 / math.factorial(13))
    for n in (11, 9, 7, 5, 3, 1):
        sign = 1.0 if n % 4 == 1 else -1.0
        acc = acc * t2 + sign / math.factorial(n)
    return acc * t


def kernel(
    prop, coords_any, momenta_any, slab, out,
    x_in, coords, momenta, send1, recv1, lt, wg, send2, recv2, lhs, wts, send3, recv3,
    in_sem, loc_sem, s1, r1, s2, r2, s3, r3, known,
):
    src = lax.axis_index("src")
    space = lax.axis_index("space")
    z = space // NQ
    q = space % NQ
    sx = src % 4
    sy = src // 4

    loads = [pltpu.make_async_copy(prop.at[:, c], x_in.at[:, c], in_sem.at[c]) for c in range(2)]
    small = [
        pltpu.make_async_copy(momenta_any, momenta, in_sem.at[3]),
        pltpu.make_async_copy(coords_any, coords, in_sem.at[4]),
    ]
    barrier = pltpu.get_barrier_semaphore()
    z_mates = [{"src": src, "space": ((z + r) % NZ) * NQ + q} for r in (1, NZ - 1, 2, NZ - 2, 4, NZ - 4)]
    q_mates = [{"src": src, "space": z * NQ + (q + r) % NQ} for r in range(1, NQ)]
    src_mates = [{"src": (src + r) % NSRC_AX, "space": space} for r in range(1, NSRC_AX)]
    first = src_mates + q_mates + z_mates[:2]
    for dev in first:
        pl.semaphore_signal(barrier, inc=1, device_id=dev, device_id_type=MESH)
    for cp in loads + small:
        cp.start()

    def tell(level, devs):
        for dev in devs:
            pl.semaphore_signal(known.at[level], inc=1, device_id=dev, device_id_type=MESH)

    lane16 = lax.broadcasted_iota(jnp.int32, (16, LANES), 1)
    for c in range(2):
        loads[c].wait()
        for t in range(NC2 // 16):
            vs = [x_in[b, c, t * 16 : t * 16 + 16, :] for b in range(8)]
            vs = swap_bits(vs, ((1, 1), (2, 2), (4, 4)), lane16)
            for d in range(8):
                row = c * NC2 + t * 16
                send1[d, row : row + 16, :] = vs[d]

    pl.semaphore_wait(barrier, len(first))

    order = ((1, 2), (1, 1), (1, 3), (0, 2), (1, 0), (0, 1), (0, 3))
    own = pltpu.make_async_copy(send1.at[src], recv1.at[src], loc_sem.at[0])
    own.start()
    sent = []
    for dy, dx in order:
        d = ((sy + dy) % 2) * 4 + (sx + dx) % 4
        cp = pltpu.make_async_remote_copy(
            src_ref=send1.at[d], dst_ref=recv1.at[src], send_sem=s1.at[d], recv_sem=r1.at[src],
            device_id={"src": d, "space": space}, device_id_type=MESH,
        )
        cp.start()
        sent.append(cp)

    tell(0, q_mates)
    tell(1, z_mates[:2])

    for cp in small:
        cp.wait()
    lane1 = lax.broadcasted_iota(jnp.int32, (1, LANES), 1)
    first_half = lane1 < NMOM
    m3 = momenta[...].astype(F32)
    m3 = jnp.concatenate([m3, m3, jnp.zeros((3, LANES - 2 * NMOM), F32)], axis=1)
    base = slab[0] + z * (NQ * LANES)
    shift_a = jnp.where(first_half, 0.0, 24.0)
    shift_b = jnp.where(first_half, 72.0, 0.0)
    rows = 64

    def phases(step, carry):
        row = lax.broadcasted_iota(jnp.int32, (rows, LANES), 0) + step * rows
        local = ((row >> 7) << 7) + (((row >> 5) & 3) << 1) + ((row >> 2) & 1) + (((row >> 3) & 3) << 3) + ((row & 3) << 5)
        site = local + base
        site = jnp.where(site >= LAT * LAT * LAT, site - LAT * LAT * LAT, site).astype(F32)
        x0 = jnp.floor((site + 0.5) * (1.0 / (LAT * LAT)))
        rest = site - x0 * (LAT * LAT)
        x1 = jnp.floor((rest + 0.5) * (1.0 / LAT))
        x2 = rest - x1 * LAT
        u = x0 * m3[0:1] + x1 * m3[1:2] + x2 * m3[2:3]
        w = jnp.concatenate([cos_steps(mod_lat(u + shift_a)), cos_steps(mod_lat(u + shift_b))], axis=1)
        wts[pl.ds(pl.multiple_of(step * rows, rows), rows), :] = w.astype(BF)
        return carry

    lax.fori_loop(0, NQ * LANES // rows, phases, 0)

    here = lax.broadcasted_iota(jnp.int32, (3, 64), 1) == space
    xyz = jnp.sum(jnp.where(here, coords[...].astype(F32), 0.0), axis=1, keepdims=True)
    u = jnp.sum(xyz * m3, axis=0, keepdims=True)
    scale = 1.0 / math.sqrt(NZ * NQ * LANES)
    cosine = cos_steps(mod_lat(u)) * scale
    sine = cos_steps(mod_lat(u + jnp.where(first_half, 24.0, 72.0))) * scale

    def take(j):
        turned = recv1[j].T
        for g in range(4):
            lt[g, pl.ds(pl.multiple_of(j * 32, 32), 32), :] = turned[g * 32 : g * 32 + 32]

    own.wait()
    take(src)
    for n, (dy, dx) in enumerate(reversed(order)):
        if n == 3:
            pl.semaphore_wait(known.at[1], 2)
            tell(2, z_mates[2:4])
        d = ((sy - dy + 2) % 2) * 4 + (sx - dx + 4) % 4
        pltpu.make_async_remote_copy(
            src_ref=send1.at[d], dst_ref=recv1.at[d], send_sem=s1.at[d], recv_sem=r1.at[d],
            device_id={"src": d, "space": space}, device_id_type=MESH,
        ).wait_recv()
        take(d)

    me = src * NQ + q
    y = 2 * sy + q // 2

    def mate(dx, dy, dc):
        at = (y + dy) % 4
        return (at // 2) * 4 + (sx + dx) % 4, (at % 2) * 2 + (q + dc) % 2

    hops = [(dx, dy, dc) for dx in range(4) for dy in range(4) for dc in range(2) if dx + dy + dc]
    hops.sort(key=lambda h: -min(h[0], 4 - h[0]) - min(h[1], 4 - h[1]))
    lane8 = (lax.broadcasted_iota(jnp.int32, (8, LANES), 1) >> 3) & 3
    picks = [lane8 == x for x in range(4)]

    for jhi in range(2):
        for t in range(K // 16):
            at = t * 16
            vs = [recv1[4 * jhi + jlo, at : at + 16, :] for jlo in range(4)]
            vs = swap_bits(vs, ((1, 32), (2, 64)), lane16)
            for g in range(4):
                wg[g, at : at + 16, :LANES] = vs[g]
                if at < NC2:
                    wg[g, NC2 + at : NC2 + at + 16, LANES:] = -vs[g]
                else:
                    wg[g, at - NC2 : at - NC2 + 16, LANES:] = vs[g]
        traces = []
        for g in range(4):
            tt = jnp.dot(lt[g], wg[g], preferred_element_type=F32)
            for i in range(8):
                parts = []
                for c in range(2):
                    acc = tt[i * 32 : i * 32 + 8, c * LANES : (c + 1) * LANES]
                    for x in range(1, 4):
                        acc = jnp.where(picks[x], tt[i * 32 + 8 * x : i * 32 + 8 * x + 8, c * LANES : (c + 1) * LANES], acc)
                    parts.append(acc)
                traces.append(jnp.concatenate(parts, axis=0).astype(BF))
        for i in range(8):
            vs = swap_bits([traces[g * 8 + i] for g in range(4)], ((1, 1), (2, 2)), lane16)
            for t in range(4):
                send2[jhi, i * NQ + t] = vs[t]
        if jhi == 0:
            pl.semaphore_wait(known.at[0], NQ - 1)
        for dx, dy, dc in hops:
            ds, dq = mate(dx, dy, dc)
            to = ds * NQ + dq
            cp = pltpu.make_async_remote_copy(
                src_ref=send2.at[jhi, to], dst_ref=recv2.at[jhi, me], send_sem=s2.at[jhi, to], recv_sem=r2.at[jhi, me],
                device_id={"src": ds, "space": z * NQ + dq}, device_id_type=MESH,
            )
            cp.start()
            sent.append(cp)
        pltpu.make_async_copy(send2.at[jhi, me], recv2.at[jhi, me], loc_sem.at[1 + jhi]).start()
        if jhi == 0:
            pl.semaphore_wait(known.at[2], 2)
            tell(3, z_mates[4:])

    for jhi in range(2):
        pltpu.make_async_copy(send2.at[jhi, me], recv2.at[jhi, me], loc_sem.at[1 + jhi]).wait()
        for dx, dy, dc in reversed(hops):
            ds, dq = mate(dx, dy, dc)
            at = ds * NQ + dq
            pltpu.make_async_remote_copy(
                src_ref=send2.at[jhi, at], dst_ref=recv2.at[jhi, at], send_sem=s2.at[jhi, at], recv_sem=r2.at[jhi, at],
                device_id={"src": ds, "space": z * NQ + dq}, device_id_type=MESH,
            ).wait_recv()
        for qq in range(NQ):
            vs = [recv2[jhi, d * NQ + qq] for d in range(8)]
            vs = swap_bits(vs, ((1, 4), (2, 32), (4, 64)), lane16)
            for b in range(8):
                lhs[b * 16 : b * 16 + 16, qq * LANES : (qq + 1) * LANES] = vs[b]
        prod = jnp.dot(lhs[...], wts[...], preferred_element_type=F32)
        for b in range(8):
            send3[8 * jhi + b] = prod[b * 16 : b * 16 + 8, :LANES] + prod[b * 16 + 8 : b * 16 + 16, LANES:]
        if jhi == 0:
            pl.semaphore_wait(known.at[3], 2)
        for b in range(8):
            to = 8 * jhi + b

            @pl.when(z != to)
            def _():
                pltpu.make_async_remote_copy(
                    src_ref=send3.at[to], dst_ref=recv3.at[z], send_sem=s3.at[to], recv_sem=r3.at[z],
                    device_id={"src": src, "space": to * NQ + q}, device_id_type=MESH,
                ).start()

            @pl.when(z == to)
            def _():
                pltpu.make_async_copy(send3.at[to], recv3.at[to], loc_sem.at[3]).start()

    for cp in sent:
        cp.wait_send()

    pltpu.make_async_copy(send3.at[z], recv3.at[z], loc_sem.at[3]).wait()
    last = []
    for r in range(1, NZ):
        at = (z + r) % NZ
        cp = pltpu.make_async_remote_copy(
            src_ref=send3.at[at], dst_ref=recv3.at[at], send_sem=s3.at[at], recv_sem=r3.at[at],
            device_id={"src": src, "space": at * NQ + q}, device_id_type=MESH,
        )
        cp.wait_recv()
        last.append(cp)
    total = recv3[0]
    for t in range(1, NZ):
        total = total + recv3[t]
    swapped = jnp.where(first_half, pltpu.roll(total, LANES - NMOM, 1), pltpu.roll(total, NMOM, 1))
    done = total * cosine + swapped * sine
    out[:, 0, 0] = done[:, :NMOM]
    out[:, 0, 1] = pltpu.roll(done, LANES - NMOM, 1)[:, :NMOM]
    for cp in last:
        cp.wait_send()


def per_device(propagators, source_coords, momenta, slab_start):
    dma = pltpu.SemaphoreType.DMA
    return pl.pallas_call(
        kernel,
        out_shape=pltpu.VMEM((8, 1, 2, NMOM), F32),
        in_specs=[pl.BlockSpec(memory_space=pltpu.HBM)] * 3 + [pl.BlockSpec(memory_space=pltpu.SMEM)],
        out_specs=pl.BlockSpec(memory_space=pltpu.VMEM),
        scratch_shapes=[
            pltpu.VMEM((8, 2, NC2, LANES), BF),
            pltpu.VMEM((3, 64), jnp.int32),
            pltpu.VMEM((3, NMOM), jnp.int32),
            pltpu.VMEM((8, K, LANES), BF),
            pltpu.VMEM((8, K, LANES), BF),
            pltpu.VMEM((4, 256, K), BF),
            pltpu.VMEM((4, K, 2 * LANES), BF),
            pltpu.VMEM((2, 32, 16, LANES), BF),
            pltpu.VMEM((2, 32, 16, LANES), BF),
            pltpu.VMEM((LANES, NQ * LANES), BF),
            pltpu.VMEM((NQ * LANES, 2 * LANES), BF),
            pltpu.VMEM((NZ, 8, LANES), F32),
            pltpu.VMEM((NZ, 8, LANES), F32),
            dma((5,)),
            dma((4,)),
            dma((8,)),
            dma((8,)),
            dma((2, 32)),
            dma((2, 32)),
            dma((16,)),
            dma((16,)),
            pltpu.SemaphoreType.REGULAR((4,)),
        ],
        compiler_params=pltpu.CompilerParams(
            collective_id=0, has_side_effects=True, vmem_limit_bytes=32 * 1024 * 1024
        ),
    )(*[pltpu.with_memory_space_constraint(x, pltpu.HBM) for x in (propagators, source_coords.T, momenta.T)], slab_start)


def solution(mesh):
    placed = (P("src", None, None, "space"), P(), P(), P())
    return jax.shard_map(
        per_device,
        mesh=mesh,
        in_specs=placed,
        out_specs=P("src", "space", None, None),
        check_vma=False,
    )
```

```python
import functools
import math

import jax
import jax.numpy as jnp
from jax import lax
from jax.experimental import pallas as pl
from jax.experimental.pallas import tpu as pltpu
from jax.sharding import PartitionSpec as P

LAT = 96
NC2 = 144
K = 2 * NC2
NMOM = 33
NSRC_AX = 8
NQ = 4
NZ = 16
LANES = 128
MESH = pl.DeviceIdType.MESH
BF = jnp.bfloat16
F32 = jnp.float32


def swap_bits(vs, bits, lane):
    vs = list(vs)
    for bit, s in bits:
        low = (lane & s) == 0
        for u in range(len(vs)):
            if u & bit:
                continue
            a, b = vs[u], vs[u | bit]
            vs[u] = jnp.where(low, a, pltpu.roll(b, s, 1))
            vs[u | bit] = jnp.where(low, pltpu.roll(a, LANES - s, 1), b)
    return vs


def mod_lat(u):
    return u - LAT * jnp.floor((u + 0.5) * (1.0 / LAT))


def cos_steps(u):
    t = (jnp.abs(u - 48.0) - 24.0) * (2.0 * math.pi / LAT)
    t2 = t * t
    acc = jnp.full_like(t, 1.0 / math.factorial(13))
    for n in (11, 9, 7, 5, 3, 1):
        sign = 1.0 if n % 4 == 1 else -1.0
        acc = acc * t2 + sign / math.factorial(n)
    return acc * t


def kernel(
    prop, coords_any, momenta_any, slab, out,
    x_in, coords, momenta, send1, recv1, lt, wg, send2, recv2, lhs, wts, send3, recv3,
    in_sem, loc_sem, s1, r1, s2, r2, s3, r3, known,
):
    src = lax.axis_index("src")
    space = lax.axis_index("space")
    z = space // NQ
    q = space % NQ
    sx = src % 4
    sy = src // 4

    loads = [pltpu.make_async_copy(prop.at[:, c], x_in.at[:, c], in_sem.at[c]) for c in range(2)]
    small = [
        pltpu.make_async_copy(momenta_any, momenta, in_sem.at[3]),
        pltpu.make_async_copy(coords_any, coords, in_sem.at[4]),
    ]
    barrier = pltpu.get_barrier_semaphore()
    z_mates = [{"src": src, "space": ((z + r) % NZ) * NQ + q} for r in (1, NZ - 1, 2, NZ - 2, 4, NZ - 4)]
    q_mates = [{"src": src, "space": z * NQ + (q + r) % NQ} for r in range(1, NQ)]
    order = ((1, 2), (1, 1), (1, 3), (0, 2), (1, 0), (0, 1), (0, 3))
    src_mates = [{"src": ((sy + dy) % 2) * 4 + (sx + dx) % 4, "space": space} for dy, dx in order]
    first = src_mates + z_mates[:2] + q_mates
    for dev in first:
        pl.semaphore_signal(barrier, inc=1, device_id=dev, device_id_type=MESH)
    for cp in loads + small:
        cp.start()

    def tell(level, devs):
        for dev in devs:
            pl.semaphore_signal(known.at[level], inc=1, device_id=dev, device_id_type=MESH)

    lane16 = lax.broadcasted_iota(jnp.int32, (16, LANES), 1)
    for c in range(2):
        loads[c].wait()
        for t in range(NC2 // 16):
            vs = [x_in[b, c, t * 16 : t * 16 + 16, :] for b in range(8)]
            vs = swap_bits(vs, ((1, 1), (2, 2), (4, 4)), lane16)
            for d in range(8):
                row = c * NC2 + t * 16
                send1[d, row : row + 16, :] = vs[d]

    pl.semaphore_wait(barrier, len(first))

    own = pltpu.make_async_copy(send1.at[src], recv1.at[src], loc_sem.at[0])
    own.start()
    sent = []
    for dy, dx in order:
        d = ((sy + dy) % 2) * 4 + (sx + dx) % 4
        cp = pltpu.make_async_remote_copy(
            src_ref=send1.at[d], dst_ref=recv1.at[src], send_sem=s1.at[d], recv_sem=r1.at[src],
            device_id={"src": d, "space": space}, device_id_type=MESH,
        )
        cp.start()
        sent.append(cp)

    tell(0, q_mates)
    tell(1, z_mates[:2])

    for cp in small:
        cp.wait()
    lane1 = lax.broadcasted_iota(jnp.int32, (1, LANES), 1)
    first_half = lane1 < NMOM
    m3 = momenta[...].astype(F32)
    m3 = jnp.concatenate([m3, m3, jnp.zeros((3, LANES - 2 * NMOM), F32)], axis=1)
    base = slab[0] + z * (NQ * LANES)
    shift_a = jnp.where(first_half, 0.0, 24.0)
    shift_b = jnp.where(first_half, 72.0, 0.0)
    rows = 64

    def phases(step, carry):
        row = lax.broadcasted_iota(jnp.int32, (rows, LANES), 0) + step * rows
        local = ((row >> 7) << 7) + (((row >> 5) & 3) << 1) + ((row >> 2) & 1) + (((row >> 3) & 3) << 3) + ((row & 3) << 5)
        site = local + base
        site = jnp.where(site >= LAT * LAT * LAT, site - LAT * LAT * LAT, site).astype(F32)
        x0 = jnp.floor((site + 0.5) * (1.0 / (LAT * LAT)))
        rest = site - x0 * (LAT * LAT)
        x1 = jnp.floor((rest + 0.5) * (1.0 / LAT))
        x2 = rest - x1 * LAT
        u = x0 * m3[0:1] + x1 * m3[1:2] + x2 * m3[2:3]
        w = jnp.concatenate([cos_steps(mod_lat(u + shift_a)), cos_steps(mod_lat(u + shift_b))], axis=1)
        wts[pl.ds(pl.multiple_of(step * rows, rows), rows), :] = w.astype(BF)
        return carry

    lax.fori_loop(0, NQ * LANES // rows, phases, 0)

    here = lax.broadcasted_iota(jnp.int32, (3, 64), 1) == space
    xyz = jnp.sum(jnp.where(here, coords[...].astype(F32), 0.0), axis=1, keepdims=True)
    u = jnp.sum(xyz * m3, axis=0, keepdims=True)
    scale = 1.0 / math.sqrt(NZ * NQ * LANES)
    cosine = cos_steps(mod_lat(u)) * scale
    sine = cos_steps(mod_lat(u + jnp.where(first_half, 24.0, 72.0))) * scale

    def take(j):
        turned = recv1[j].T
        for g in range(4):
            lt[g, pl.ds(pl.multiple_of(j * 32, 32), 32), :] = turned[g * 32 : g * 32 + 32]

    own.wait()
    take(src)
    for n, (dy, dx) in enumerate(order):
        if n == 0:
            pl.semaphore_wait(known.at[1], 2)
            tell(2, z_mates[2:4])
        if n == 3:
            pl.semaphore_wait(known.at[2], 2)
            tell(3, z_mates[4:])
        d = ((sy - dy + 2) % 2) * 4 + (sx - dx + 4) % 4
        pltpu.make_async_remote_copy(
            src_ref=send1.at[d], dst_ref=recv1.at[d], send_sem=s1.at[d], recv_sem=r1.at[d],
            device_id={"src": d, "space": space}, device_id_type=MESH,
        ).wait_recv()
        take(d)

    me = src * NQ + q
    y = 2 * sy + q // 2

    def mate(dx, dy, dc):
        at = (y + dy) % 4
        return (at // 2) * 4 + (sx + dx) % 4, (at % 2) * 2 + (q + dc) % 2

    hops = [(dx, dy, dc) for dx in range(4) for dy in range(4) for dc in range(2) if dx + dy + dc]
    hops.sort(key=lambda h: -min(h[0], 4 - h[0]) - min(h[1], 4 - h[1]))
    lane8 = (lax.broadcasted_iota(jnp.int32, (8, LANES), 1) >> 3) & 3
    picks = [lane8 == x for x in range(4)]

    def send_traces(jhi):
        for dx, dy, dc in hops:
            ds, dq = mate(dx, dy, dc)
            to = ds * NQ + dq
            cp = pltpu.make_async_remote_copy(
                src_ref=send2.at[jhi, to], dst_ref=recv2.at[jhi, me], send_sem=s2.at[jhi, to], recv_sem=r2.at[jhi, me],
                device_id={"src": ds, "space": z * NQ + dq}, device_id_type=MESH,
            )
            cp.start()
            sent.append(cp)
        pltpu.make_async_copy(send2.at[jhi, me], recv2.at[jhi, me], loc_sem.at[1 + jhi]).start()

    def traces_here(jhi, some):
        for dx, dy, dc in some:
            ds, dq = mate(dx, dy, dc)
            at = ds * NQ + dq
            pltpu.make_async_remote_copy(
                src_ref=send2.at[jhi, at], dst_ref=recv2.at[jhi, at], send_sem=s2.at[jhi, at], recv_sem=r2.at[jhi, at],
                device_id={"src": ds, "space": z * NQ + dq}, device_id_type=MESH,
            ).wait_recv()

    for jhi in range(2):
        for t in range(K // 16):
            at = t * 16
            vs = [recv1[4 * jhi + jlo, at : at + 16, :] for jlo in range(4)]
            vs = swap_bits(vs, ((1, 32), (2, 64)), lane16)
            for g in range(4):
                wg[g, at : at + 16, :LANES] = vs[g]
                if at < NC2:
                    wg[g, NC2 + at : NC2 + at + 16, LANES:] = -vs[g]
                else:
                    wg[g, at - NC2 : at - NC2 + 16, LANES:] = vs[g]
        traces = []
        for g in range(4):
            tt = jnp.dot(lt[g], wg[g], preferred_element_type=F32)
            for i in range(8):
                parts = []
                for c in range(2):
                    acc = tt[i * 32 : i * 32 + 8, c * LANES : (c + 1) * LANES]
                    for x in range(1, 4):
                        acc = jnp.where(picks[x], tt[i * 32 + 8 * x : i * 32 + 8 * x + 8, c * LANES : (c + 1) * LANES], acc)
                    parts.append(acc)
                traces.append(jnp.concatenate(parts, axis=0).astype(BF))
        for i in range(8):
            vs = swap_bits([traces[g * 8 + i] for g in range(4)], ((1, 1), (2, 2)), lane16)
            for t in range(4):
                send2[jhi, i * NQ + t] = vs[t]
        if jhi == 0:
            pl.semaphore_wait(known.at[0], NQ - 1)
            send_traces(0)

    for jhi in range(2):
        pltpu.make_async_copy(send2.at[jhi, me], recv2.at[jhi, me], loc_sem.at[1 + jhi]).wait()
        near_first = hops[::-1]
        if jhi == 0:
            traces_here(0, near_first[:1])
            send_traces(1)
            traces_here(0, near_first[1:])
        else:
            traces_here(1, near_first)
        for qq in range(NQ):
            vs = [recv2[jhi, d * NQ + qq] for d in range(8)]
            vs = swap_bits(vs, ((1, 4), (2, 32), (4, 64)), lane16)
            for b in range(8):
                lhs[b * 16 : b * 16 + 16, qq * LANES : (qq + 1) * LANES] = vs[b]
        prod = jnp.dot(lhs[...], wts[...], preferred_element_type=F32)
        for b in range(8):
            send3[8 * jhi + b] = prod[b * 16 : b * 16 + 8, :LANES] + prod[b * 16 + 8 : b * 16 + 16, LANES:]
        if jhi == 0:
            pl.semaphore_wait(known.at[3], 2)
        for b in range(8):
            to = 8 * jhi + b

            @pl.when(z != to)
            def _():
                pltpu.make_async_remote_copy(
                    src_ref=send3.at[to], dst_ref=recv3.at[z], send_sem=s3.at[to], recv_sem=r3.at[z],
                    device_id={"src": src, "space": to * NQ + q}, device_id_type=MESH,
                ).start()

            @pl.when(z == to)
            def _():
                pltpu.make_async_copy(send3.at[to], recv3.at[to], loc_sem.at[3]).start()

    for cp in sent:
        cp.wait_send()

    pltpu.make_async_copy(send3.at[z], recv3.at[z], loc_sem.at[3]).wait()
    last = []
    for r in range(1, NZ):
        at = (z + r) % NZ
        cp = pltpu.make_async_remote_copy(
            src_ref=send3.at[at], dst_ref=recv3.at[at], send_sem=s3.at[at], recv_sem=r3.at[at],
            device_id={"src": src, "space": at * NQ + q}, device_id_type=MESH,
        )
        last.append(cp)
    for cp in last:
        cp.wait_send()
    for cp in last:
        cp.wait_recv()
    total = recv3[0]
    for t in range(1, NZ):
        total = total + recv3[t]
    swapped = jnp.where(first_half, pltpu.roll(total, LANES - NMOM, 1), pltpu.roll(total, NMOM, 1))
    done = total * cosine + swapped * sine
    out[:, 0, 0] = done[:, :NMOM]
    out[:, 0, 1] = pltpu.roll(done, LANES - NMOM, 1)[:, :NMOM]


def per_device(propagators, source_coords, momenta, slab_start):
    dma = pltpu.SemaphoreType.DMA
    return pl.pallas_call(
        kernel,
        out_shape=pltpu.VMEM((8, 1, 2, NMOM), F32),
        in_specs=[pl.BlockSpec(memory_space=pltpu.HBM)] * 3 + [pl.BlockSpec(memory_space=pltpu.SMEM)],
        out_specs=pl.BlockSpec(memory_space=pltpu.VMEM),
        scratch_shapes=[
            pltpu.VMEM((8, 2, NC2, LANES), BF),
            pltpu.VMEM((3, 64), jnp.int32),
            pltpu.VMEM((3, NMOM), jnp.int32),
            pltpu.VMEM((8, K, LANES), BF),
            pltpu.VMEM((8, K, LANES), BF),
            pltpu.VMEM((4, 256, K), BF),
            pltpu.VMEM((4, K, 2 * LANES), BF),
            pltpu.VMEM((2, 32, 16, LANES), BF),
            pltpu.VMEM((2, 32, 16, LANES), BF),
            pltpu.VMEM((LANES, NQ * LANES), BF),
            pltpu.VMEM((NQ * LANES, 2 * LANES), BF),
            pltpu.VMEM((NZ, 8, LANES), F32),
            pltpu.VMEM((NZ, 8, LANES), F32),
            dma((5,)),
            dma((4,)),
            dma((8,)),
            dma((8,)),
            dma((2, 32)),
            dma((2, 32)),
            dma((16,)),
            dma((16,)),
            pltpu.SemaphoreType.REGULAR((4,)),
        ],
        compiler_params=pltpu.CompilerParams(
            collective_id=0, has_side_effects=True, vmem_limit_bytes=32 * 1024 * 1024
        ),
    )(*[pltpu.with_memory_space_constraint(x, pltpu.HBM) for x in (propagators, source_coords.T, momenta.T)], slab_start)


def solution(mesh):
    placed = (P("src", None, None, "space"), P(), P(), P())
    return jax.shard_map(
        per_device,
        mesh=mesh,
        in_specs=placed,
        out_specs=P("src", "space", None, None),
        check_vma=False,
    )
```

```python
import functools
import math

import jax
import jax.numpy as jnp
from jax import lax
from jax.experimental import pallas as pl
from jax.experimental.pallas import tpu as pltpu
from jax.sharding import PartitionSpec as P

LAT = 96
NC2 = 144
K = 2 * NC2
NMOM = 33
NSRC_AX = 8
NQ = 4
NZ = 16
LANES = 128
MESH = pl.DeviceIdType.MESH
BF = jnp.bfloat16
F32 = jnp.float32


def swap_bits(vs, bits, lane):
    vs = list(vs)
    for bit, s in bits:
        low = (lane & s) == 0
        for u in range(len(vs)):
            if u & bit:
                continue
            a, b = vs[u], vs[u | bit]
            vs[u] = jnp.where(low, a, pltpu.roll(b, s, 1))
            vs[u | bit] = jnp.where(low, pltpu.roll(a, LANES - s, 1), b)
    return vs


def mod_lat(u):
    return u - LAT * jnp.floor((u + 0.5) * (1.0 / LAT))


def cos_steps(u):
    t = (jnp.abs(u - 48.0) - 24.0) * (2.0 * math.pi / LAT)
    t2 = t * t
    acc = jnp.full_like(t, 1.0 / math.factorial(13))
    for n in (11, 9, 7, 5, 3, 1):
        sign = 1.0 if n % 4 == 1 else -1.0
        acc = acc * t2 + sign / math.factorial(n)
    return acc * t


def kernel(
    prop, coords_any, momenta_any, slab, out,
    x_in, coords, momenta, mid, send1, recv1, send2, recv2, lhs, wts, send3, recv3,
    in_sem, loc_sem, s1, r1, s2, r2, s3, r3, known,
):
    src = lax.axis_index("src")
    space = lax.axis_index("space")
    z = space // NQ
    q = space % NQ
    sx = src % 4
    sy = src // 4

    loads = [pltpu.make_async_copy(prop.at[:, c], x_in.at[:, c], in_sem.at[c]) for c in range(2)]
    small = [
        pltpu.make_async_copy(momenta_any, momenta, in_sem.at[3]),
        pltpu.make_async_copy(coords_any, coords, in_sem.at[4]),
    ]
    barrier = pltpu.get_barrier_semaphore()
    z_mates = [{"src": src, "space": ((z + r) % NZ) * NQ + q} for r in (1, NZ - 1, 2, NZ - 2, 4, NZ - 4)]
    q_mates = [{"src": src, "space": z * NQ + (q + r) % NQ} for r in range(1, NQ)]
    order = ((1, 2), (1, 1), (1, 3), (0, 2), (1, 0), (0, 1), (0, 3))
    src_mates = [{"src": ((sy + dy) % 2) * 4 + (sx + dx) % 4, "space": space} for dy, dx in order]
    first = src_mates + z_mates[:2] + q_mates
    for dev in first:
        pl.semaphore_signal(barrier, inc=1, device_id=dev, device_id_type=MESH)
    for cp in loads + small:
        cp.start()

    def tell(level, devs):
        for dev in devs:
            pl.semaphore_signal(known.at[level], inc=1, device_id=dev, device_id_type=MESH)

    lane16 = lax.broadcasted_iota(jnp.int32, (16, LANES), 1)
    for c in range(2):
        loads[c].wait()
        for t in range(NC2 // 16):
            vs = [x_in[b, c, t * 16 : t * 16 + 16, :] for b in range(8)]
            vs = swap_bits(vs, ((1, 1), (2, 2), (4, 4)), lane16)
            for d in range(8):
                row = c * NC2 + t * 16
                mid[d, row : row + 16, :] = vs[d]

    def turn(d, carry):
        block = mid[d]
        send1[d, :LANES] = block[:LANES].T
        send1[d, LANES : 2 * LANES] = block[NC2 : NC2 + LANES].T
        rest = jnp.concatenate([block[LANES:NC2], block[NC2 + LANES :]], axis=0)
        rest = jnp.concatenate([rest] + [pltpu.roll(rest, LANES - 32 * g, 1) for g in (1, 2, 3)], axis=0)
        send1[d, 2 * LANES :] = rest.T[:32]
        return carry

    lax.fori_loop(0, NSRC_AX, turn, 0)

    pl.semaphore_wait(barrier, len(first))

    own = pltpu.make_async_copy(send1.at[src], recv1.at[src], loc_sem.at[0])
    own.start()
    sent = []
    for dy, dx in order:
        d = ((sy + dy) % 2) * 4 + (sx + dx) % 4
        cp = pltpu.make_async_remote_copy(
            src_ref=send1.at[d], dst_ref=recv1.at[src], send_sem=s1.at[d], recv_sem=r1.at[src],
            device_id={"src": d, "space": space}, device_id_type=MESH,
        )
        cp.start()
        sent.append(cp)

    tell(0, q_mates)
    tell(1, z_mates[:2])

    for cp in small:
        cp.wait()
    lane1 = lax.broadcasted_iota(jnp.int32, (1, LANES), 1)
    first_half = lane1 < NMOM
    m3 = momenta[...].astype(F32)
    m3 = jnp.concatenate([m3, m3, jnp.zeros((3, LANES - 2 * NMOM), F32)], axis=1)
    base = slab[0] + z * (NQ * LANES)
    shift_a = jnp.where(first_half, 0.0, 24.0)
    shift_b = jnp.where(first_half, 72.0, 0.0)
    rows = 64

    def phases(step, carry):
        row = lax.broadcasted_iota(jnp.int32, (rows, LANES), 0) + step * rows
        local = ((row >> 7) << 7) + (((row >> 5) & 3) << 1) + ((row >> 2) & 1) + (((row >> 3) & 3) << 3) + ((row & 3) << 5)
        site = local + base
        site = jnp.where(site >= LAT * LAT * LAT, site - LAT * LAT * LAT, site).astype(F32)
        x0 = jnp.floor((site + 0.5) * (1.0 / (LAT * LAT)))
        rest = site - x0 * (LAT * LAT)
        x1 = jnp.floor((rest + 0.5) * (1.0 / LAT))
        x2 = rest - x1 * LAT
        u = x0 * m3[0:1] + x1 * m3[1:2] + x2 * m3[2:3]
        w = jnp.concatenate([cos_steps(mod_lat(u + shift_a)), cos_steps(mod_lat(u + shift_b))], axis=1)
        wts[pl.ds(pl.multiple_of(step * rows, rows), rows), :] = w.astype(BF)
        return carry

    lax.fori_loop(0, NQ * LANES // rows, phases, 0)

    here = lax.broadcasted_iota(jnp.int32, (3, 64), 1) == space
    xyz = jnp.sum(jnp.where(here, coords[...].astype(F32), 0.0), axis=1, keepdims=True)
    u = jnp.sum(xyz * m3, axis=0, keepdims=True)
    scale = 1.0 / math.sqrt(NZ * NQ * LANES)
    cosine = cos_steps(mod_lat(u)) * scale
    sine = cos_steps(mod_lat(u + jnp.where(first_half, 24.0, 72.0))) * scale

    own.wait()
    for n, (dy, dx) in enumerate(order):
        if n == 0:
            pl.semaphore_wait(known.at[1], 2)
            tell(2, z_mates[2:4])
        if n == 3:
            pl.semaphore_wait(known.at[2], 2)
            tell(3, z_mates[4:])
        d = ((sy - dy + 2) % 2) * 4 + (sx - dx + 4) % 4
        pltpu.make_async_remote_copy(
            src_ref=send1.at[d], dst_ref=recv1.at[d], send_sem=s1.at[d], recv_sem=r1.at[d],
            device_id={"src": d, "space": space}, device_id_type=MESH,
        ).wait_recv()

    me = src * NQ + q
    y = 2 * sy + q // 2

    def mate(dx, dy, dc):
        at = (y + dy) % 4
        return (at // 2) * 4 + (sx + dx) % 4, (at % 2) * 2 + (q + dc) % 2

    hops = [(dx, dy, dc) for dx in range(4) for dy in range(4) for dc in range(2) if dx + dy + dc]
    hops.sort(key=lambda h: -min(h[0], 4 - h[0]) - min(h[1], 4 - h[1]))
    lane8 = (lax.broadcasted_iota(jnp.int32, (8, LANES), 1) >> 3) & 3
    picks = [lane8 == x for x in range(4)]
    lane_l = lax.broadcasted_iota(jnp.int32, (2 * LANES, LANES), 1)
    lane_r = lax.broadcasted_iota(jnp.int32, (LANES, LANES), 1)

    def send_traces(jhi):
        for dx, dy, dc in hops:
            ds, dq = mate(dx, dy, dc)
            to = ds * NQ + dq
            cp = pltpu.make_async_remote_copy(
                src_ref=send2.at[jhi, to], dst_ref=recv2.at[jhi, me], send_sem=s2.at[jhi, to], recv_sem=r2.at[jhi, me],
                device_id={"src": ds, "space": z * NQ + dq}, device_id_type=MESH,
            )
            cp.start()
            sent.append(cp)
        pltpu.make_async_copy(send2.at[jhi, me], recv2.at[jhi, me], loc_sem.at[1 + jhi]).start()

    def traces_here(jhi, some):
        for dx, dy, dc in some:
            ds, dq = mate(dx, dy, dc)
            at = ds * NQ + dq
            pltpu.make_async_remote_copy(
                src_ref=send2.at[jhi, at], dst_ref=recv2.at[jhi, at], send_sem=s2.at[jhi, at], recv_sem=r2.at[jhi, at],
                device_id={"src": ds, "space": z * NQ + dq}, device_id_type=MESH,
            ).wait_recv()

    for jhi in range(2):
        traces = []
        for g in range(4):
            def rows_of(blocks, part):
                at = part * LANES + (32 * g if part < 2 else 0)
                return jnp.concatenate([recv1[k, at : at + 32, :] for k in blocks], axis=0)

            left = [rows_of(range(8), part) for part in range(3)]
            left[2] = jnp.where((lane_l >> 5) == g, left[2], jnp.zeros_like(left[2]))
            b0, b1, b2 = [rows_of(range(4 * jhi, 4 * jhi + 4), part) for part in range(3)]
            b2t = jnp.where((lane_r & 16) == 0, pltpu.roll(b2, LANES - 16, 1), -pltpu.roll(b2, 16, 1))
            right = jnp.concatenate(
                [jnp.concatenate([b0, b1, b2], axis=1), jnp.concatenate([b1, -b0, b2t], axis=1)], axis=0
            )
            tt = lax.dot_general(
                jnp.concatenate(left, axis=1), right, (((1,), (1,)), ((), ())), preferred_element_type=F32
            )
            for i in range(8):
                parts = []
                for c in range(2):
                    acc = tt[i * 32 : i * 32 + 8, c * LANES : (c + 1) * LANES]
                    for x in range(1, 4):
                        acc = jnp.where(picks[x], tt[i * 32 + 8 * x : i * 32 + 8 * x + 8, c * LANES : (c + 1) * LANES], acc)
                    parts.append(acc)
                traces.append(jnp.concatenate(parts, axis=0).astype(BF))
        for i in range(8):
            vs = swap_bits([traces[g * 8 + i] for g in range(4)], ((1, 1), (2, 2)), lane16)
            for t in range(4):
                send2[jhi, i * NQ + t] = vs[t]
        if jhi == 0:
            pl.semaphore_wait(known.at[0], NQ - 1)
            send_traces(0)

    for jhi in range(2):
        pltpu.make_async_copy(send2.at[jhi, me], recv2.at[jhi, me], loc_sem.at[1 + jhi]).wait()
        near_first = hops[::-1]
        if jhi == 0:
            traces_here(0, near_first[:3])
            send_traces(1)
            traces_here(0, near_first[3:])
        else:
            traces_here(1, near_first)
        for qq in range(NQ):
            vs = [recv2[jhi, d * NQ + qq] for d in range(8)]
            vs = swap_bits(vs, ((1, 4), (2, 32), (4, 64)), lane16)
            for b in range(8):
                lhs[b * 16 : b * 16 + 16, qq * LANES : (qq + 1) * LANES] = vs[b]
        prod = jnp.dot(lhs[...], wts[...], preferred_element_type=F32)
        for b in range(8):
            send3[8 * jhi + b] = prod[b * 16 : b * 16 + 8, :LANES] + prod[b * 16 + 8 : b * 16 + 16, LANES:]
        if jhi == 0:
            pl.semaphore_wait(known.at[3], 2)
        for b in range(8):
            to = 8 * jhi + b

            @pl.when(z != to)
            def _():
                pltpu.make_async_remote_copy(
                    src_ref=send3.at[to], dst_ref=recv3.at[z], send_sem=s3.at[to], recv_sem=r3.at[z],
                    device_id={"src": src, "space": to * NQ + q}, device_id_type=MESH,
                ).start()

            @pl.when(z == to)
            def _():
                pltpu.make_async_copy(send3.at[to], recv3.at[to], loc_sem.at[3]).start()

    for cp in sent:
        cp.wait_send()

    pltpu.make_async_copy(send3.at[z], recv3.at[z], loc_sem.at[3]).wait()
    last = []
    for r in range(1, NZ):
        at = (z + r) % NZ
        cp = pltpu.make_async_remote_copy(
            src_ref=send3.at[at], dst_ref=recv3.at[at], send_sem=s3.at[at], recv_sem=r3.at[at],
            device_id={"src": src, "space": at * NQ + q}, device_id_type=MESH,
        )
        last.append(cp)
    for cp in last:
        cp.wait_send()
    for cp in last:
        cp.wait_recv()
    total = recv3[0]
    for t in range(1, NZ):
        total = total + recv3[t]
    swapped = jnp.where(first_half, pltpu.roll(total, LANES - NMOM, 1), pltpu.roll(total, NMOM, 1))
    done = total * cosine + swapped * sine
    out[:, 0, 0] = done[:, :NMOM]
    out[:, 0, 1] = pltpu.roll(done, LANES - NMOM, 1)[:, :NMOM]


def per_device(propagators, source_coords, momenta, slab_start):
    dma = pltpu.SemaphoreType.DMA
    return pl.pallas_call(
        kernel,
        out_shape=pltpu.VMEM((8, 1, 2, NMOM), F32),
        in_specs=[pl.BlockSpec(memory_space=pltpu.HBM)] * 3 + [pl.BlockSpec(memory_space=pltpu.SMEM)],
        out_specs=pl.BlockSpec(memory_space=pltpu.VMEM),
        scratch_shapes=[
            pltpu.VMEM((8, 2, NC2, LANES), BF),
            pltpu.VMEM((3, 64), jnp.int32),
            pltpu.VMEM((3, NMOM), jnp.int32),
            pltpu.VMEM((8, K, LANES), BF),
            pltpu.VMEM((8, K, LANES), BF),
            pltpu.VMEM((8, K, LANES), BF),
            pltpu.VMEM((2, 32, 16, LANES), BF),
            pltpu.VMEM((2, 32, 16, LANES), BF),
            pltpu.VMEM((LANES, NQ * LANES), BF),
            pltpu.VMEM((NQ * LANES, 2 * LANES), BF),
            pltpu.VMEM((NZ, 8, LANES), F32),
            pltpu.VMEM((NZ, 8, LANES), F32),
            dma((5,)),
            dma((4,)),
            dma((8,)),
            dma((8,)),
            dma((2, 32)),
            dma((2, 32)),
            dma((16,)),
            dma((16,)),
            pltpu.SemaphoreType.REGULAR((4,)),
        ],
        compiler_params=pltpu.CompilerParams(
            collective_id=0, has_side_effects=True, vmem_limit_bytes=32 * 1024 * 1024
        ),
    )(*[pltpu.with_memory_space_constraint(x, pltpu.HBM) for x in (propagators, source_coords.T, momenta.T)], slab_start)


def solution(mesh):
    placed = (P("src", None, None, "space"), P(), P(), P())
    return jax.shard_map(
        per_device,
        mesh=mesh,
        in_specs=placed,
        out_specs=P("src", "space", None, None),
        check_vma=False,
    )
```

```python
import functools
import math

import jax
import jax.numpy as jnp
from jax import lax
from jax.experimental import pallas as pl
from jax.experimental.pallas import tpu as pltpu
from jax.sharding import PartitionSpec as P

LAT = 96
NC2 = 144
K = 2 * NC2
NMOM = 33
NSRC_AX = 8
NQ = 4
NZ = 16
LANES = 128
MESH = pl.DeviceIdType.MESH
BF = jnp.bfloat16
F32 = jnp.float32


def swap_bits(vs, bits, lane):
    vs = list(vs)
    for bit, s in bits:
        low = (lane & s) == 0
        for u in range(len(vs)):
            if u & bit:
                continue
            a, b = vs[u], vs[u | bit]
            vs[u] = jnp.where(low, a, pltpu.roll(b, s, 1))
            vs[u | bit] = jnp.where(low, pltpu.roll(a, LANES - s, 1), b)
    return vs


def mod_lat(u):
    return u - LAT * jnp.floor((u + 0.5) * (1.0 / LAT))


def cos_steps(u):
    t = (jnp.abs(u - 48.0) - 24.0) * (2.0 * math.pi / LAT)
    t2 = t * t
    acc = jnp.full_like(t, 1.0 / math.factorial(13))
    for n in (11, 9, 7, 5, 3, 1):
        sign = 1.0 if n % 4 == 1 else -1.0
        acc = acc * t2 + sign / math.factorial(n)
    return acc * t


def kernel(
    prop, coords_any, momenta_any, slab, out,
    x_in, coords, momenta, mid, send1, recv1, send2, recv2, lhs, wts, send3, recv3,
    in_sem, loc_sem, s1, r1, s2, r2, s3, r3, known,
):
    src = lax.axis_index("src")
    space = lax.axis_index("space")
    z = space // NQ
    q = space % NQ
    sx = src % 4
    sy = src // 4

    loads = [pltpu.make_async_copy(prop.at[:, c], x_in.at[:, c], in_sem.at[c]) for c in range(2)]
    small = [
        pltpu.make_async_copy(momenta_any, momenta, in_sem.at[3]),
        pltpu.make_async_copy(coords_any, coords, in_sem.at[4]),
    ]
    barrier = pltpu.get_barrier_semaphore()
    z_mates = [{"src": src, "space": ((z + r) % NZ) * NQ + q} for r in (1, NZ - 1, 2, NZ - 2, 4, NZ - 4)]
    q_mates = [{"src": src, "space": z * NQ + (q + r) % NQ} for r in range(1, NQ)]
    order = ((1, 2), (1, 1), (1, 3), (0, 2), (1, 0), (0, 1), (0, 3))
    src_mates = [{"src": ((sy + dy) % 2) * 4 + (sx + dx) % 4, "space": space} for dy, dx in order]
    first = src_mates + z_mates[:2] + q_mates
    for dev in first:
        pl.semaphore_signal(barrier, inc=1, device_id=dev, device_id_type=MESH)
    for cp in loads + small:
        cp.start()

    def tell(level, devs):
        for dev in devs:
            pl.semaphore_signal(known.at[level], inc=1, device_id=dev, device_id_type=MESH)

    lane16 = lax.broadcasted_iota(jnp.int32, (16, LANES), 1)
    for c in range(2):
        loads[c].wait()
        for t in range(NC2 // 16):
            vs = [x_in[b, c, t * 16 : t * 16 + 16, :] for b in range(8)]
            vs = swap_bits(vs, ((1, 1), (2, 2), (4, 4)), lane16)
            for d in range(8):
                row = c * NC2 + t * 16
                mid[d, row : row + 16, :] = vs[d]

    def turn(d, into):
        block = mid[d]
        into[d, :LANES] = block[:LANES].T
        into[d, LANES : 2 * LANES] = block[NC2 : NC2 + LANES].T
        rest = jnp.concatenate([block[LANES:NC2], block[NC2 + LANES :]], axis=0)
        rest = jnp.concatenate([rest] + [pltpu.roll(rest, LANES - 32 * g, 1) for g in (1, 2, 3)], axis=0)
        into[d, 2 * LANES :] = rest.T[:32]

    for dy, dx in order[:3]:
        turn(((sy + dy) % 2) * 4 + (sx + dx) % 4, send1)

    pl.semaphore_wait(barrier, len(first))

    sent = []
    for n, (dy, dx) in enumerate(order):
        d = ((sy + dy) % 2) * 4 + (sx + dx) % 4
        if n >= 3:
            turn(d, send1)
        cp = pltpu.make_async_remote_copy(
            src_ref=send1.at[d], dst_ref=recv1.at[src], send_sem=s1.at[d], recv_sem=r1.at[src],
            device_id={"src": d, "space": space}, device_id_type=MESH,
        )
        cp.start()
        sent.append(cp)

    turn(src, recv1)

    tell(0, q_mates)
    tell(1, z_mates[:2])

    for cp in small:
        cp.wait()
    lane1 = lax.broadcasted_iota(jnp.int32, (1, LANES), 1)
    first_half = lane1 < NMOM
    m3 = momenta[...].astype(F32)
    m3 = jnp.concatenate([m3, m3, jnp.zeros((3, LANES - 2 * NMOM), F32)], axis=1)
    base = slab[0] + z * (NQ * LANES)
    shift_a = jnp.where(first_half, 0.0, 24.0)
    shift_b = jnp.where(first_half, 72.0, 0.0)
    rows = 64

    def phases(step, carry):
        row = lax.broadcasted_iota(jnp.int32, (rows, LANES), 0) + step * rows
        local = ((row >> 7) << 7) + (((row >> 5) & 3) << 1) + ((row >> 2) & 1) + (((row >> 3) & 3) << 3) + ((row & 3) << 5)
        site = local + base
        site = jnp.where(site >= LAT * LAT * LAT, site - LAT * LAT * LAT, site).astype(F32)
        x0 = jnp.floor((site + 0.5) * (1.0 / (LAT * LAT)))
        rest = site - x0 * (LAT * LAT)
        x1 = jnp.floor((rest + 0.5) * (1.0 / LAT))
        x2 = rest - x1 * LAT
        u = x0 * m3[0:1] + x1 * m3[1:2] + x2 * m3[2:3]
        w = jnp.concatenate([cos_steps(mod_lat(u + shift_a)), cos_steps(mod_lat(u + shift_b))], axis=1)
        wts[pl.ds(pl.multiple_of(step * rows, rows), rows), :] = w.astype(BF)
        return carry

    lax.fori_loop(0, NQ * LANES // rows, phases, 0)

    here = lax.broadcasted_iota(jnp.int32, (3, 64), 1) == space
    xyz = jnp.sum(jnp.where(here, coords[...].astype(F32), 0.0), axis=1, keepdims=True)
    u = jnp.sum(xyz * m3, axis=0, keepdims=True)
    scale = 1.0 / math.sqrt(NZ * NQ * LANES)
    cosine = cos_steps(mod_lat(u)) * scale
    sine = cos_steps(mod_lat(u + jnp.where(first_half, 24.0, 72.0))) * scale

    for n, (dy, dx) in enumerate(order):
        if n == 0:
            pl.semaphore_wait(known.at[1], 2)
            tell(2, z_mates[2:4])
        if n == 3:
            pl.semaphore_wait(known.at[2], 2)
            tell(3, z_mates[4:])
        d = ((sy - dy + 2) % 2) * 4 + (sx - dx + 4) % 4
        pltpu.make_async_remote_copy(
            src_ref=send1.at[d], dst_ref=recv1.at[d], send_sem=s1.at[d], recv_sem=r1.at[d],
            device_id={"src": d, "space": space}, device_id_type=MESH,
        ).wait_recv()

    me = src * NQ + q
    y = 2 * sy + q // 2

    def mate(dx, dy, dc):
        at = (y + dy) % 4
        return (at // 2) * 4 + (sx + dx) % 4, (at % 2) * 2 + (q + dc) % 2

    hops = [(dx, dy, dc) for dx in range(4) for dy in range(4) for dc in range(2) if dx + dy + dc]
    hops.sort(key=lambda h: -min(h[0], 4 - h[0]) - min(h[1], 4 - h[1]))
    lane8 = (lax.broadcasted_iota(jnp.int32, (8, LANES), 1) >> 3) & 3
    picks = [lane8 == x for x in range(4)]
    lane_l = lax.broadcasted_iota(jnp.int32, (2 * LANES, LANES), 1)
    lane_r = lax.broadcasted_iota(jnp.int32, (LANES, LANES), 1)

    def send_traces(jhi):
        for dx, dy, dc in hops:
            ds, dq = mate(dx, dy, dc)
            to = ds * NQ + dq
            cp = pltpu.make_async_remote_copy(
                src_ref=send2.at[jhi, to], dst_ref=recv2.at[jhi, me], send_sem=s2.at[jhi, to], recv_sem=r2.at[jhi, me],
                device_id={"src": ds, "space": z * NQ + dq}, device_id_type=MESH,
            )
            cp.start()
            sent.append(cp)
        pltpu.make_async_copy(send2.at[jhi, me], recv2.at[jhi, me], loc_sem.at[1 + jhi]).start()

    def traces_here(jhi, some):
        for dx, dy, dc in some:
            ds, dq = mate(dx, dy, dc)
            at = ds * NQ + dq
            pltpu.make_async_remote_copy(
                src_ref=send2.at[jhi, at], dst_ref=recv2.at[jhi, at], send_sem=s2.at[jhi, at], recv_sem=r2.at[jhi, at],
                device_id={"src": ds, "space": z * NQ + dq}, device_id_type=MESH,
            ).wait_recv()

    for jhi in range(2):
        traces = []
        for g in range(4):
            def rows_of(blocks, part):
                at = part * LANES + (32 * g if part < 2 else 0)
                return jnp.concatenate([recv1[k, at : at + 32, :] for k in blocks], axis=0)

            left = [rows_of(range(8), part) for part in range(3)]
            left[2] = jnp.where((lane_l >> 5) == g, left[2], jnp.zeros_like(left[2]))
            b0, b1, b2 = [rows_of(range(4 * jhi, 4 * jhi + 4), part) for part in range(3)]
            b2t = jnp.where((lane_r & 16) == 0, pltpu.roll(b2, LANES - 16, 1), -pltpu.roll(b2, 16, 1))
            right = jnp.concatenate(
                [jnp.concatenate([b0, b1, b2], axis=1), jnp.concatenate([b1, -b0, b2t], axis=1)], axis=0
            )
            tt = lax.dot_general(
                jnp.concatenate(left, axis=1), right, (((1,), (1,)), ((), ())), preferred_element_type=F32
            )
            for i in range(8):
                parts = []
                for c in range(2):
                    acc = tt[i * 32 : i * 32 + 8, c * LANES : (c + 1) * LANES]
                    for x in range(1, 4):
                        acc = jnp.where(picks[x], tt[i * 32 + 8 * x : i * 32 + 8 * x + 8, c * LANES : (c + 1) * LANES], acc)
                    parts.append(acc)
                traces.append(jnp.concatenate(parts, axis=0).astype(BF))
        for i in range(8):
            vs = swap_bits([traces[g * 8 + i] for g in range(4)], ((1, 1), (2, 2)), lane16)
            for t in range(4):
                send2[jhi, i * NQ + t] = vs[t]
        if jhi == 0:
            pl.semaphore_wait(known.at[0], NQ - 1)
            send_traces(0)

    for jhi in range(2):
        pltpu.make_async_copy(send2.at[jhi, me], recv2.at[jhi, me], loc_sem.at[1 + jhi]).wait()
        near_first = hops[::-1]
        if jhi == 0:
            traces_here(0, near_first[:3])
            send_traces(1)
            traces_here(0, near_first[3:])
        else:
            traces_here(1, near_first)
        for qq in range(NQ):
            vs = [recv2[jhi, d * NQ + qq] for d in range(8)]
            vs = swap_bits(vs, ((1, 4), (2, 32), (4, 64)), lane16)
            for b in range(8):
                lhs[b * 16 : b * 16 + 16, qq * LANES : (qq + 1) * LANES] = vs[b]
        prod = jnp.dot(lhs[...], wts[...], preferred_element_type=F32)
        for b in range(8):
            send3[8 * jhi + b] = prod[b * 16 : b * 16 + 8, :LANES] + prod[b * 16 + 8 : b * 16 + 16, LANES:]
        if jhi == 0:
            pl.semaphore_wait(known.at[3], 2)
        for b in range(8):
            to = 8 * jhi + b

            @pl.when(z != to)
            def _():
                pltpu.make_async_remote_copy(
                    src_ref=send3.at[to], dst_ref=recv3.at[z], send_sem=s3.at[to], recv_sem=r3.at[z],
                    device_id={"src": src, "space": to * NQ + q}, device_id_type=MESH,
                ).start()

            @pl.when(z == to)
            def _():
                pltpu.make_async_copy(send3.at[to], recv3.at[to], loc_sem.at[3]).start()

    for cp in sent:
        cp.wait_send()

    pltpu.make_async_copy(send3.at[z], recv3.at[z], loc_sem.at[3]).wait()
    last = []
    for r in range(1, NZ):
        at = (z + r) % NZ
        cp = pltpu.make_async_remote_copy(
            src_ref=send3.at[at], dst_ref=recv3.at[at], send_sem=s3.at[at], recv_sem=r3.at[at],
            device_id={"src": src, "space": at * NQ + q}, device_id_type=MESH,
        )
        last.append(cp)
    for cp in last:
        cp.wait_send()
    for cp in last:
        cp.wait_recv()
    total = recv3[0]
    for t in range(1, NZ):
        total = total + recv3[t]
    swapped = jnp.where(first_half, pltpu.roll(total, LANES - NMOM, 1), pltpu.roll(total, NMOM, 1))
    done = total * cosine + swapped * sine
    out[:, 0, 0] = done[:, :NMOM]
    out[:, 0, 1] = pltpu.roll(done, LANES - NMOM, 1)[:, :NMOM]


def per_device(propagators, source_coords, momenta, slab_start):
    dma = pltpu.SemaphoreType.DMA
    return pl.pallas_call(
        kernel,
        out_shape=pltpu.VMEM((8, 1, 2, NMOM), F32),
        in_specs=[pl.BlockSpec(memory_space=pltpu.HBM)] * 3 + [pl.BlockSpec(memory_space=pltpu.SMEM)],
        out_specs=pl.BlockSpec(memory_space=pltpu.VMEM),
        scratch_shapes=[
            pltpu.VMEM((8, 2, NC2, LANES), BF),
            pltpu.VMEM((3, 64), jnp.int32),
            pltpu.VMEM((3, NMOM), jnp.int32),
            pltpu.VMEM((8, K, LANES), BF),
            pltpu.VMEM((8, K, LANES), BF),
            pltpu.VMEM((8, K, LANES), BF),
            pltpu.VMEM((2, 32, 16, LANES), BF),
            pltpu.VMEM((2, 32, 16, LANES), BF),
            pltpu.VMEM((LANES, NQ * LANES), BF),
            pltpu.VMEM((NQ * LANES, 2 * LANES), BF),
            pltpu.VMEM((NZ, 8, LANES), F32),
            pltpu.VMEM((NZ, 8, LANES), F32),
            dma((5,)),
            dma((4,)),
            dma((8,)),
            dma((8,)),
            dma((2, 32)),
            dma((2, 32)),
            dma((16,)),
            dma((16,)),
            pltpu.SemaphoreType.REGULAR((4,)),
        ],
        compiler_params=pltpu.CompilerParams(
            collective_id=0, has_side_effects=True, vmem_limit_bytes=32 * 1024 * 1024
        ),
    )(*[pltpu.with_memory_space_constraint(x, pltpu.HBM) for x in (propagators, source_coords.T, momenta.T)], slab_start)


def solution(mesh):
    placed = (P("src", None, None, "space"), P(), P(), P())
    return jax.shard_map(
        per_device,
        mesh=mesh,
        in_specs=placed,
        out_specs=P("src", "space", None, None),
        check_vma=False,
    )
```

```python
import functools
import math

import jax
import jax.numpy as jnp
from jax import lax
from jax.experimental import pallas as pl
from jax.experimental.pallas import tpu as pltpu
from jax.sharding import PartitionSpec as P

LAT = 96
NC2 = 144
K = 2 * NC2
NMOM = 33
NSRC_AX = 8
NQ = 4
NZ = 16
LANES = 128
MESH = pl.DeviceIdType.MESH
BF = jnp.bfloat16
F32 = jnp.float32


def swap_bits(vs, bits, lane):
    vs = list(vs)
    for bit, s in bits:
        low = (lane & s) == 0
        for u in range(len(vs)):
            if u & bit:
                continue
            a, b = vs[u], vs[u | bit]
            vs[u] = jnp.where(low, a, pltpu.roll(b, s, 1))
            vs[u | bit] = jnp.where(low, pltpu.roll(a, LANES - s, 1), b)
    return vs


def mod_lat(u):
    return u - LAT * jnp.floor((u + 0.5) * (1.0 / LAT))


def cos_steps(u):
    t = (jnp.abs(u - 48.0) - 24.0) * (2.0 * math.pi / LAT)
    t2 = t * t
    acc = jnp.full_like(t, 1.0 / math.factorial(13))
    for n in (11, 9, 7, 5, 3, 1):
        sign = 1.0 if n % 4 == 1 else -1.0
        acc = acc * t2 + sign / math.factorial(n)
    return acc * t


def kernel(
    prop, coords_any, momenta_any, slab, out,
    x_in, coords, momenta, mid, send1, recv1, send2, recv2, lhs, wts, send3, recv3,
    in_sem, loc_sem, s1, r1, s2, r2, s3, r3, known,
):
    src = lax.axis_index("src")
    space = lax.axis_index("space")
    z = space // NQ
    q = space % NQ
    sx = src % 4
    sy = src // 4

    loads = [pltpu.make_async_copy(prop.at[:, c], x_in.at[:, c], in_sem.at[c]) for c in range(2)]
    small = [
        pltpu.make_async_copy(momenta_any, momenta, in_sem.at[3]),
        pltpu.make_async_copy(coords_any, coords, in_sem.at[4]),
    ]
    barrier = pltpu.get_barrier_semaphore()
    z_mates = [{"src": src, "space": ((z + r) % NZ) * NQ + q} for r in (1, NZ - 1, 2, NZ - 2, 4, NZ - 4)]
    q_mates = [{"src": src, "space": z * NQ + (q + r) % NQ} for r in range(1, NQ)]
    order = ((1, 2), (1, 1), (1, 3), (0, 2), (1, 0), (0, 1), (0, 3))
    src_mates = [{"src": ((sy + dy) % 2) * 4 + (sx + dx) % 4, "space": space} for dy, dx in order]
    first = src_mates + z_mates[:2] + q_mates
    for dev in first:
        pl.semaphore_signal(barrier, inc=1, device_id=dev, device_id_type=MESH)
    for cp in loads + small:
        cp.start()

    def tell(level, devs):
        for dev in devs:
            pl.semaphore_signal(known.at[level], inc=1, device_id=dev, device_id_type=MESH)

    lane16 = lax.broadcasted_iota(jnp.int32, (16, LANES), 1)
    for c in range(2):
        loads[c].wait()
        for t in range(NC2 // 16):
            vs = [x_in[b, c, t * 16 : t * 16 + 16, :] for b in range(8)]
            vs = swap_bits(vs, ((1, 1), (2, 2), (4, 4)), lane16)
            for d in range(8):
                row = c * NC2 + t * 16
                mid[d, row : row + 16, :] = vs[d]

    def turn(d, into):
        block = mid[d]
        into[d, :LANES] = block[:LANES].T
        into[d, LANES : 2 * LANES] = block[NC2 : NC2 + LANES].T
        rest = jnp.concatenate([block[LANES:NC2], block[NC2 + LANES :]], axis=0)
        rest = jnp.concatenate([rest] + [pltpu.roll(rest, LANES - 32 * g, 1) for g in (1, 2, 3)], axis=0)
        into[d, 2 * LANES :] = rest.T[:32]

    for dy, dx in order[:1]:
        turn(((sy + dy) % 2) * 4 + (sx + dx) % 4, send1)

    pl.semaphore_wait(barrier, len(first))

    sent = []
    for n, (dy, dx) in enumerate(order):
        d = ((sy + dy) % 2) * 4 + (sx + dx) % 4
        if n >= 1:
            turn(d, send1)
        cp = pltpu.make_async_remote_copy(
            src_ref=send1.at[d], dst_ref=recv1.at[src], send_sem=s1.at[d], recv_sem=r1.at[src],
            device_id={"src": d, "space": space}, device_id_type=MESH,
        )
        cp.start()
        sent.append(cp)

    turn(src, recv1)

    tell(0, q_mates)
    tell(1, z_mates[:2])

    for cp in small:
        cp.wait()
    lane1 = lax.broadcasted_iota(jnp.int32, (1, LANES), 1)
    first_half = lane1 < NMOM
    m3 = momenta[...].astype(F32)
    m3 = jnp.concatenate([m3, m3, jnp.zeros((3, LANES - 2 * NMOM), F32)], axis=1)
    base = slab[0] + z * (NQ * LANES)
    shift_a = jnp.where(first_half, 0.0, 24.0)
    shift_b = jnp.where(first_half, 72.0, 0.0)
    rows = 64

    def phases(step, carry):
        row = lax.broadcasted_iota(jnp.int32, (rows, LANES), 0) + step * rows
        local = ((row >> 7) << 7) + (((row >> 5) & 3) << 1) + ((row >> 2) & 1) + (((row >> 3) & 3) << 3) + ((row & 3) << 5)
        site = local + base
        site = jnp.where(site >= LAT * LAT * LAT, site - LAT * LAT * LAT, site).astype(F32)
        x0 = jnp.floor((site + 0.5) * (1.0 / (LAT * LAT)))
        rest = site - x0 * (LAT * LAT)
        x1 = jnp.floor((rest + 0.5) * (1.0 / LAT))
        x2 = rest - x1 * LAT
        u = x0 * m3[0:1] + x1 * m3[1:2] + x2 * m3[2:3]
        w = jnp.concatenate([cos_steps(mod_lat(u + shift_a)), cos_steps(mod_lat(u + shift_b))], axis=1)
        wts[pl.ds(pl.multiple_of(step * rows, rows), rows), :] = w.astype(BF)
        return carry

    lax.fori_loop(0, NQ * LANES // rows, phases, 0)

    here = lax.broadcasted_iota(jnp.int32, (3, 64), 1) == space
    xyz = jnp.sum(jnp.where(here, coords[...].astype(F32), 0.0), axis=1, keepdims=True)
    u = jnp.sum(xyz * m3, axis=0, keepdims=True)
    scale = 1.0 / math.sqrt(NZ * NQ * LANES)
    cosine = cos_steps(mod_lat(u)) * scale
    sine = cos_steps(mod_lat(u + jnp.where(first_half, 24.0, 72.0))) * scale

    for n, (dy, dx) in enumerate(order):
        if n == 0:
            pl.semaphore_wait(known.at[1], 2)
            tell(2, z_mates[2:4])
        if n == 3:
            pl.semaphore_wait(known.at[2], 2)
            tell(3, z_mates[4:])
        d = ((sy - dy + 2) % 2) * 4 + (sx - dx + 4) % 4
        pltpu.make_async_remote_copy(
            src_ref=send1.at[d], dst_ref=recv1.at[d], send_sem=s1.at[d], recv_sem=r1.at[d],
            device_id={"src": d, "space": space}, device_id_type=MESH,
        ).wait_recv()

    me = src * NQ + q
    y = 2 * sy + q // 2

    def mate(dx, dy, dc):
        at = (y + dy) % 4
        return (at // 2) * 4 + (sx + dx) % 4, (at % 2) * 2 + (q + dc) % 2

    hops = [(dx, dy, dc) for dx in range(4) for dy in range(4) for dc in range(2) if dx + dy + dc]
    hops.sort(key=lambda h: -min(h[0], 4 - h[0]) - min(h[1], 4 - h[1]))
    lane8 = (lax.broadcasted_iota(jnp.int32, (8, LANES), 1) >> 3) & 3
    picks = [lane8 == x for x in range(4)]
    lane_l = lax.broadcasted_iota(jnp.int32, (2 * LANES, LANES), 1)
    lane_r = lax.broadcasted_iota(jnp.int32, (LANES, LANES), 1)

    def send_traces(jhi):
        for dx, dy, dc in hops:
            ds, dq = mate(dx, dy, dc)
            to = ds * NQ + dq
            cp = pltpu.make_async_remote_copy(
                src_ref=send2.at[jhi, to], dst_ref=recv2.at[jhi, me], send_sem=s2.at[jhi, to], recv_sem=r2.at[jhi, me],
                device_id={"src": ds, "space": z * NQ + dq}, device_id_type=MESH,
            )
            cp.start()
            sent.append(cp)
        pltpu.make_async_copy(send2.at[jhi, me], recv2.at[jhi, me], loc_sem.at[1 + jhi]).start()

    def traces_here(jhi, some):
        for dx, dy, dc in some:
            ds, dq = mate(dx, dy, dc)
            at = ds * NQ + dq
            pltpu.make_async_remote_copy(
                src_ref=send2.at[jhi, at], dst_ref=recv2.at[jhi, at], send_sem=s2.at[jhi, at], recv_sem=r2.at[jhi, at],
                device_id={"src": ds, "space": z * NQ + dq}, device_id_type=MESH,
            ).wait_recv()

    for jhi in range(2):
        traces = []
        for g in range(4):
            def rows_of(blocks, part):
                at = part * LANES + (32 * g if part < 2 else 0)
                return jnp.concatenate([recv1[k, at : at + 32, :] for k in blocks], axis=0)

            left = [rows_of(range(8), part) for part in range(3)]
            left[2] = jnp.where((lane_l >> 5) == g, left[2], jnp.zeros_like(left[2]))
            b0, b1, b2 = [rows_of(range(4 * jhi, 4 * jhi + 4), part) for part in range(3)]
            b2t = jnp.where((lane_r & 16) == 0, pltpu.roll(b2, LANES - 16, 1), -pltpu.roll(b2, 16, 1))
            right = jnp.concatenate(
                [jnp.concatenate([b0, b1, b2], axis=1), jnp.concatenate([b1, -b0, b2t], axis=1)], axis=0
            )
            tt = lax.dot_general(
                jnp.concatenate(left, axis=1), right, (((1,), (1,)), ((), ())), preferred_element_type=F32
            )
            for i in range(8):
                parts = []
                for c in range(2):
                    acc = tt[i * 32 : i * 32 + 8, c * LANES : (c + 1) * LANES]
                    for x in range(1, 4):
                        acc = jnp.where(picks[x], tt[i * 32 + 8 * x : i * 32 + 8 * x + 8, c * LANES : (c + 1) * LANES], acc)
                    parts.append(acc)
                traces.append(jnp.concatenate(parts, axis=0).astype(BF))
        for i in range(8):
            vs = swap_bits([traces[g * 8 + i] for g in range(4)], ((1, 1), (2, 2)), lane16)
            for t in range(4):
                send2[jhi, i * NQ + t] = vs[t]
        if jhi == 0:
            pl.semaphore_wait(known.at[0], NQ - 1)
            send_traces(0)

    for jhi in range(2):
        pltpu.make_async_copy(send2.at[jhi, me], recv2.at[jhi, me], loc_sem.at[1 + jhi]).wait()
        near_first = hops[::-1]
        if jhi == 0:
            traces_here(0, near_first[:3])
            send_traces(1)
            traces_here(0, near_first[3:])
        else:
            traces_here(1, near_first)
        for qq in range(NQ):
            vs = [recv2[jhi, d * NQ + qq] for d in range(8)]
            vs = swap_bits(vs, ((1, 4), (2, 32), (4, 64)), lane16)
            for b in range(8):
                lhs[b * 16 : b * 16 + 16, qq * LANES : (qq + 1) * LANES] = vs[b]
        prod = jnp.dot(lhs[...], wts[...], preferred_element_type=F32)
        for b in range(8):
            send3[8 * jhi + b] = prod[b * 16 : b * 16 + 8, :LANES] + prod[b * 16 + 8 : b * 16 + 16, LANES:]
        if jhi == 0:
            pl.semaphore_wait(known.at[3], 2)
        for b in range(8):
            to = 8 * jhi + b

            @pl.when(z != to)
            def _():
                pltpu.make_async_remote_copy(
                    src_ref=send3.at[to], dst_ref=recv3.at[z], send_sem=s3.at[to], recv_sem=r3.at[z],
                    device_id={"src": src, "space": to * NQ + q}, device_id_type=MESH,
                ).start()

            @pl.when(z == to)
            def _():
                pltpu.make_async_copy(send3.at[to], recv3.at[to], loc_sem.at[3]).start()

    for cp in sent:
        cp.wait_send()

    pltpu.make_async_copy(send3.at[z], recv3.at[z], loc_sem.at[3]).wait()
    last = []
    for r in range(1, NZ):
        at = (z + r) % NZ
        cp = pltpu.make_async_remote_copy(
            src_ref=send3.at[at], dst_ref=recv3.at[at], send_sem=s3.at[at], recv_sem=r3.at[at],
            device_id={"src": src, "space": at * NQ + q}, device_id_type=MESH,
        )
        last.append(cp)
    for cp in last:
        cp.wait_send()
    for cp in last:
        cp.wait_recv()
    total = recv3[0]
    for t in range(1, NZ):
        total = total + recv3[t]
    swapped = jnp.where(first_half, pltpu.roll(total, LANES - NMOM, 1), pltpu.roll(total, NMOM, 1))
    done = total * cosine + swapped * sine
    out[:, 0, 0] = done[:, :NMOM]
    out[:, 0, 1] = pltpu.roll(done, LANES - NMOM, 1)[:, :NMOM]


def per_device(propagators, source_coords, momenta, slab_start):
    dma = pltpu.SemaphoreType.DMA
    return pl.pallas_call(
        kernel,
        out_shape=pltpu.VMEM((8, 1, 2, NMOM), F32),
        in_specs=[pl.BlockSpec(memory_space=pltpu.HBM)] * 3 + [pl.BlockSpec(memory_space=pltpu.SMEM)],
        out_specs=pl.BlockSpec(memory_space=pltpu.VMEM),
        scratch_shapes=[
            pltpu.VMEM((8, 2, NC2, LANES), BF),
            pltpu.VMEM((3, 64), jnp.int32),
            pltpu.VMEM((3, NMOM), jnp.int32),
            pltpu.VMEM((8, K, LANES), BF),
            pltpu.VMEM((8, K, LANES), BF),
            pltpu.VMEM((8, K, LANES), BF),
            pltpu.VMEM((2, 32, 16, LANES), BF),
            pltpu.VMEM((2, 32, 16, LANES), BF),
            pltpu.VMEM((LANES, NQ * LANES), BF),
            pltpu.VMEM((NQ * LANES, 2 * LANES), BF),
            pltpu.VMEM((NZ, 8, LANES), F32),
            pltpu.VMEM((NZ, 8, LANES), F32),
            dma((5,)),
            dma((4,)),
            dma((8,)),
            dma((8,)),
            dma((2, 32)),
            dma((2, 32)),
            dma((16,)),
            dma((16,)),
            pltpu.SemaphoreType.REGULAR((4,)),
        ],
        compiler_params=pltpu.CompilerParams(
            collective_id=0, has_side_effects=True, vmem_limit_bytes=32 * 1024 * 1024
        ),
    )(*[pltpu.with_memory_space_constraint(x, pltpu.HBM) for x in (propagators, source_coords.T, momenta.T)], slab_start)


def solution(mesh):
    placed = (P("src", None, None, "space"), P(), P(), P())
    return jax.shard_map(
        per_device,
        mesh=mesh,
        in_specs=placed,
        out_specs=P("src", "space", None, None),
        check_vma=False,
    )
```
